32 devices in a mesh: dp: 8 (over y, x, core), tensor: 4 (over z).
Axes of the slice: x: 2, y: 2, z: 4, core: 2. Of those that a mesh axis runs over, the one named last changes fastest.
Arguments:
- image_in: bfloat16 [2, 4, 1024, 1536], P(None, 'tensor', 'dp'), may hold values from -6 to 6
- text_in: bfloat16 [2, 4, 160, 1536], P(None, 'tensor', 'dp'), may hold values from -6 to 6
- cond_table: float32 [8, 1536], replicated, may hold values from -6 to 6
- cond_index: int32 [2, 4], replicated, may hold values from 0 to 7
- w_mod: bfloat16 [2, 2, 1536, 9216], P(None, None, 'dp', 'tensor'), may hold values from -0.21875 to 0.21875
- w_qkv: bfloat16 [2, 2, 3, 1536, 1536], P(None, None, None, 'dp', 'tensor'), may hold values from -0.15625 to 0.15625
- w_out: bfloat16 [2, 2, 1536, 1536], P(None, None, 'tensor', 'dp'), may hold values from -0.875 to 0.875
- w_up: bfloat16 [2, 2, 1536, 6144], P(None, None, 'dp', 'tensor'), may hold values from -0.15625 to 0.15625
- w_down: bfloat16 [2, 2, 6144, 1536], P(None, None, 'tensor', 'dp'), may hold values from -0.078125 to 0.078125
- cot_image: bfloat16 [2, 4, 1024, 1536], P(None, 'tensor', 'dp'), may hold values from -6 to 6
- cot_text: bfloat16 [2, 4, 160, 1536], P(None, 'tensor', 'dp'), may hold values from -6 to 6
Outputs:
- image_out: bfloat16 [2, 4, 1024, 1536], P(None, 'tensor', 'dp')
- text_out: bfloat16 [2, 4, 160, 1536], P(None, 'tensor', 'dp')
- grad_image: float32 [2, 4, 1024, 1536], P(None, 'tensor', 'dp')
- grad_text: float32 [2, 4, 160, 1536], P(None, 'tensor', 'dp')
- grad_cond: float32 [8, 1536], P(None, 'dp')
- grad_w_mod: float32 [2, 2, 1536, 9216], P(None, None, 'dp', 'tensor')
- grad_w_qkv: float32 [2, 2, 3, 1536, 1536], P(None, None, None, 'dp', 'tensor')
- grad_w_out: float32 [2, 2, 1536, 1536], P(None, None, 'tensor', 'dp')
- grad_w_up: float32 [2, 2, 1536, 6144], P(None, None, 'dp', 'tensor')
- grad_w_down: float32 [2, 2, 6144, 1536], P(None, None, 'tensor', 'dp')
The draws below stay inside these ranges and needn't reach their ends.
All inputs are finite; a program needn't handle non-finite values.
Results may differ from the reference program's by a relative error of at most 0.029.
Values may be sent and summed in bfloat16 or wider, within the bound.
No kernel may reach another device: no remote copies, remote signals or barrier semaphores. Data moves between devices by JAX's collectives and lax.ppermute only.
A program may use at most 512 MiB of HBM per device.

```python
import jax
import jax.numpy as jnp
from jax import lax

D = 1536
HEADS = 24
HDIM = 64
FF = 6144
LI = 1024
LT = 160
MB = 2
LAYERS = 2
NCOND = 8
SEQ_MB = 4
SEQS = 8


def set_ends(values, rng, smallest, high):
    index_at = [jax.random.randint(jax.random.fold_in(rng, axis), (), 0, length) for axis, length in enumerate(values.shape)]
    main_axis = values.shape.index(max(values.shape))
    next_to = index_at[:main_axis] + [(index_at[main_axis] + 1) % values.shape[main_axis]] + index_at[main_axis + 1:]
    return values.at[tuple(index_at)].set(smallest).at[tuple(next_to)].set(high)


def strengthened(values, rng, source, target, shards_of, factor):
    def block_of(axis_at):
        return (jnp.arange(values.shape[axis_at]) // (values.shape[axis_at] // shards_of)).reshape((-1,) + (1,) * (values.ndim - 1 - axis_at))

    first = jax.random.permutation(rng, shards_of)[block_of(target)]
    other_side = (block_of(target) + shards_of // 2) % shards_of
    return jnp.where((block_of(source) == first) | (block_of(source) == other_side), factor * values, values)


def levels(own_key, extent, pieces, least, top_value):
    factor_of, own = 1.0, jax.random.fold_in(own_key, 6)
    for dim, parts in pieces:
        heights = jnp.exp(jax.random.uniform(jax.random.fold_in(own, dim), (parts,), jnp.float32, least / len(pieces), top_value / len(pieces)))
        factor_of = factor_of * jnp.repeat(heights, extent[dim] // parts).reshape([-1 if axis == dim else 1 for axis in range(len(extent))])
    return factor_of


def normal_values(rng, shape, scale, bound, pieces=(), held_as=jnp.bfloat16):
    drawn = scale * jax.random.normal(rng, shape, jnp.float32)
    if pieces:
        drawn = drawn * levels(rng, shape, pieces, -0.22, 0.18)
    return jnp.clip(drawn, -bound, bound).astype(held_as)


def gaussian_with(key, dims, width, reach, shards, heavy, kind=jnp.bfloat16):
    drawn = width * jax.random.normal(key, dims, jnp.float32)
    if shards:
        drawn = drawn * levels(key, dims, shards, -0.22, 0.18)
    return jnp.clip(strengthened(drawn, jax.random.fold_in(key, 3), *heavy), -reach, reach).astype(kind)


def setup_inputs(seed: int = 0) -> dict:
    streams_of = jax.random.split(jax.random.key(seed), 12)
    return {
        "image_in": normal_values(streams_of[0], (MB, SEQ_MB, LI, D), 1.0, 6.0, ((1, 4), (2, 8))),
        "text_in": normal_values(streams_of[1], (MB, SEQ_MB, LT, D), 1.0, 6.0, ((1, 4), (2, 8))),
        "cond_table": normal_values(streams_of[2], (NCOND, D), 1.0, 6.0, (), jnp.float32),
        "cond_index": set_ends(jax.random.randint(streams_of[3], (MB, SEQ_MB), 0, NCOND), jax.random.fold_in(streams_of[3], 1), 0, NCOND - 1).astype(jnp.int32),
        "w_mod": gaussian_with(streams_of[4], (LAYERS, 2, D, 6 * D), D ** -0.5, 0.21875, ((2, 8), (3, 4)), (3, 2, 8, 2.0)),
        "w_qkv": normal_values(streams_of[5], (LAYERS, 2, 3, D, D), D ** -0.5, 0.15625, ((3, 8), (4, 4))),
        "w_out": normal_values(streams_of[6], (LAYERS, 2, D, D), (D // 32) ** -0.5, 0.875, ((2, 4), (3, 8))),
        "w_up": normal_values(streams_of[7], (LAYERS, 2, D, FF), D ** -0.5, 0.15625, ((2, 8), (3, 4))),
        "w_down": normal_values(streams_of[8], (LAYERS, 2, FF, D), FF ** -0.5, 0.078125, ((2, 4), (3, 8))),
        "cot_image": normal_values(streams_of[9], (MB, SEQ_MB, LI, D), 1.0, 6.0, ((1, 4), (2, 8))),
        "cot_text": normal_values(streams_of[10], (MB, SEQ_MB, LT, D), 1.0, 6.0, ((1, 4), (2, 8))),
    }


@jax.custom_vjp
def low(v):
    return lax.optimization_barrier(v.astype(jnp.bfloat16)).astype(jnp.float32)

@jax.custom_vjp
def low_back(v):
    return v

def low_keep(v):
    return (low(v), None)

def low_pass(kept, grad):
    return (grad,)

def back_keep(v):
    return (v, None)

def back_low(kept, grad):
    return (low(grad),)
low.defvjp(low_keep, low_pass)
low_back.defvjp(back_keep, back_low)
EPS = 1e-06

def matmul(left, right):
    return jnp.dot(left, right, precision=lax.Precision.HIGHEST, preferred_element_type=jnp.float32)

def normalize(values_in, shift_row, scale_row):
    centre = lax.optimization_barrier(jnp.mean(values_in, axis=-1, keepdims=True))
    offsets = values_in - centre
    spread = lax.optimization_barrier(jnp.mean(offsets * offsets, axis=-1, keepdims=True))
    return offsets * lax.rsqrt(spread + EPS) * (1.0 + scale_row) + shift_row

def project(normed, weight):
    return low_back(low(matmul(normed, weight)))

def one_layer(streams, mod_rows, qkv_w, out_w, up_w, down_w):
    normed = [low(normalize(streams[stream], mod_rows[stream, 0], mod_rows[stream, 1])) for stream in range(2)]
    triples = [[project(normed[stream], qkv_w[stream, part_at]) for part_at in range(3)] for stream in range(2)]
    queries = jnp.concatenate([triples[0][0], triples[1][0]], axis=0).reshape(LI + LT, HEADS, HDIM)
    all_keys = jnp.concatenate([triples[0][1], triples[1][1]], axis=0).reshape(LI + LT, HEADS, HDIM)
    values = jnp.concatenate([triples[0][2], triples[1][2]], axis=0).reshape(LI + LT, HEADS, HDIM)
    scores = low_back(jnp.einsum('qhe,khe->hqk', queries, all_keys, precision=lax.Precision.HIGHEST, preferred_element_type=jnp.float32)) * HDIM ** (-0.5)
    soft_probs = jax.nn.softmax(scores, axis=-1)
    mixed_heads = jnp.einsum('hqk,khe->qhe', low(soft_probs), values, precision=lax.Precision.HIGHEST, preferred_element_type=jnp.float32)
    mixed_heads = low_back(low(mixed_heads)).reshape(LI + LT, D)
    attn_out = [low_back(matmul(mixed_heads[:LI], out_w[0])), low_back(matmul(mixed_heads[LI:], out_w[1]))]
    result = []
    for stream in range(2):
        middle = streams[stream] + mod_rows[stream, 2] * attn_out[stream]
        normed_two = low(normalize(middle, mod_rows[stream, 3], mod_rows[stream, 4]))
        up_proj = low_back(matmul(normed_two, up_w[stream]))
        active = low(jax.nn.gelu(up_proj, approximate=True))
        result.append(middle + mod_rows[stream, 5] * low_back(matmul(active, down_w[stream])))
    return result

def reference(image_in, text_in, cond_table, cond_index, w_mod, w_qkv, w_out, w_up, w_down, cot_image, cot_text):

    def forward(mod_w, qkv_w, out_w, up_w, down_w, image_rows, text_rows, cond_rows):
        index_flat = cond_index.reshape(-1).astype(jnp.int32)
        onehot = (index_flat[:, None] == jnp.arange(NCOND, dtype=jnp.int32)[None, :]).astype(jnp.float32)
        silu_all = low(jax.nn.silu(matmul(onehot, cond_rows)))

        def sequence(packed):
            image_one, text_one, silu_one = packed
            streams = [image_one, text_one]
            for layer_at in range(LAYERS):
                mod_rows = jnp.stack([matmul(silu_one[None, :], mod_w[layer_at, stream]).reshape(6, D) for stream in range(2)])
                streams = one_layer(streams, mod_rows, qkv_w[layer_at], out_w[layer_at], up_w[layer_at], down_w[layer_at])
            return (streams[0], streams[1])
        image_res, text_res = lax.map(jax.checkpoint(sequence), (image_rows.reshape(SEQS, LI, D), text_rows.reshape(SEQS, LT, D), silu_all))
        return (image_res.reshape(image_rows.shape), text_res.reshape(text_rows.shape))
    (image_res, text_res), pullback = jax.vjp(forward, w_mod.astype(jnp.float32), w_qkv.astype(jnp.float32), w_out.astype(jnp.float32), w_up.astype(jnp.float32), w_down.astype(jnp.float32), image_in.astype(jnp.float32), text_in.astype(jnp.float32), cond_table.astype(jnp.float32))
    gradients = pullback((cot_image.astype(jnp.float32), cot_text.astype(jnp.float32)))
    return (image_res.astype(jnp.bfloat16), text_res.astype(jnp.bfloat16), gradients[5], gradients[6], gradients[7], gradients[0], gradients[1], gradients[2], gradients[3], gradients[4])
```

```python
import functools

import jax
import jax.numpy as jnp
from jax import lax
from jax.experimental import pallas as pl
from jax.experimental.layout import Layout, with_layout_constraint
from jax.experimental.pallas import tpu as pltpu
from jax.sharding import PartitionSpec as P

HDIM = 64
LANES = 128
EPS = 1e-06
HIGHEST = lax.Precision.HIGHEST
BF16 = jnp.bfloat16
F32 = jnp.float32


def dot32(pattern, left, right):
    return jnp.einsum(pattern, left, right, preferred_element_type=F32)


def tensor_swap(values, distance):
    count = lax.axis_size("tensor")
    return lax.ppermute(values, "tensor", [(i, i ^ distance) for i in range(count)])


def pair_swap(values):
    return tensor_swap(values, 1)


def hi_swap(values, block):
    return tensor_swap(values, 2 * block)


def pair_sum(own_part, other_part):
    return own_part + pair_swap(other_part.astype(BF16)).astype(F32)


def dp_sum(values):
    count = lax.axis_size("dp")
    step = 1
    while step < count:
        values = values + lax.ppermute(values, "dp", [(i, i ^ step) for i in range(count)])
        step *= 2
    return values


def rows_of_all(values):
    count = lax.axis_size("tensor")
    return jnp.stack([values] + [tensor_swap(values, at) for at in range(1, count)])


def sum_of_all(parts):
    total = parts[0]
    for at in range(1, lax.axis_size("tensor")):
        total = total + tensor_swap(parts[at].astype(BF16), at).astype(F32)
    return total


def to_sequences(parts, blocks):
    received = [parts[:2]] + [
        hi_swap(parts[2 * block : 2 * block + 2], block) for block in range(1, blocks)
    ]
    return [flat_pairs(part) for part in received]


def to_blocks(by_block, seqs):
    split = [part.reshape(2, seqs, *part.shape[1:]) for part in by_block]
    parts = [split[0]] + [hi_swap(split[block], block) for block in range(1, len(split))]
    return jnp.concatenate(parts, axis=0)


def flat_pairs(values):
    return values.reshape(-1, *values.shape[2:])


def head_mask(rows, which):
    lane = lax.broadcasted_iota(jnp.int32, (rows, LANES), 1)
    return (lane < HDIM) if which == 0 else (lane >= HDIM)


def nt_dot(left, right):
    return lax.dot_general(left, right, (((1,), (1,)), ((), ())), preferred_element_type=F32)


def attn_fwd_kernel(q_ref, k_ref, v_ref, o_ref, lse_ref):
    rows = q_ref.shape[0]
    queries = q_ref[...] * jnp.asarray(HDIM ** (-0.5), BF16)
    keys = k_ref[...]
    values_t = v_ref[...].astype(F32).T.astype(BF16)
    parts = []
    for which in range(2):
        masked = jnp.where(head_mask(rows, which), queries, jnp.zeros_like(queries))
        scores = nt_dot(keys, masked)
        peak = jnp.max(scores, axis=0, keepdims=True)
        raised = jnp.exp(scores - peak)
        total = jnp.sum(raised, axis=0, keepdims=True)
        out_t = jnp.dot(
            values_t[which * HDIM : (which + 1) * HDIM],
            raised.astype(BF16),
            preferred_element_type=F32,
        )
        parts.append(out_t * (1.0 / total))
        lse_ref[0, 0, which : which + 1, :] = peak + jnp.log(total)
    o_ref[...] = jnp.concatenate(parts, axis=0).T.astype(BF16)


def attn_bwd_kernel(q_ref, k_ref, v_ref, do_ref, lse_ref, dq_ref, dk_ref, dv_ref, dk_acc, dv_acc):
    tile = pl.program_id(1)
    rows = q_ref.shape[0]
    scale = HDIM ** (-0.5)

    @pl.when(tile == 0)
    def _():
        dk_acc[...] = jnp.zeros_like(dk_acc)
        dv_acc[...] = jnp.zeros_like(dv_acc)

    queries = q_ref[...] * jnp.asarray(scale, BF16)
    d_out = do_ref[...]
    keys = k_ref[...]
    values = v_ref[...]
    keys_t = keys.astype(F32).T.astype(BF16)
    parts = []
    for which in range(2):
        mask = head_mask(rows, which)
        q_masked = jnp.where(mask, queries, jnp.zeros_like(queries))
        do_masked = jnp.where(mask, d_out, jnp.zeros_like(d_out))
        scores = nt_dot(keys, q_masked)
        probs = jnp.exp(scores - lse_ref[0, 0, which : which + 1, :])
        d_probs = nt_dot(values, do_masked)
        centre = jnp.sum(probs * d_probs, axis=0, keepdims=True)
        d_scores = (probs * (d_probs - centre)).astype(BF16)
        dv_acc[...] += jnp.dot(probs.astype(BF16), do_masked, preferred_element_type=F32)
        dk_acc[...] += jnp.dot(d_scores, q_masked, preferred_element_type=F32)
        parts.append(
            jnp.dot(
                keys_t[which * HDIM : (which + 1) * HDIM], d_scores, preferred_element_type=F32
            )
        )
    dq_ref[...] = (jnp.concatenate(parts, axis=0).T * scale).astype(BF16)

    @pl.when(tile == pl.num_programs(1) - 1)
    def _():
        dk_ref[...] = dk_acc[...].astype(BF16)
        dv_ref[...] = dv_acc[...].astype(BF16)


def query_rows(length):
    return length // 2 if length % 32 == 0 else length


def padded_columns(columns):
    return -(-columns // LANES) * LANES


def pad_heads(packed, pieces):
    columns = packed.shape[1] // pieces
    wide = padded_columns(columns)
    if wide == columns:
        return packed
    split = packed.reshape(packed.shape[0], pieces, columns)
    return jnp.pad(split, ((0, 0), (0, 0), (0, wide - columns))).reshape(
        packed.shape[0], pieces * wide
    )


def attention_forward(packed):
    length = packed.shape[0]
    columns = packed.shape[1] // 3
    wide = padded_columns(columns)
    pairs = wide // LANES
    rows = query_rows(length)
    tiles = length // rows
    packed = pad_heads(packed, 3)
    mixed, lse = pl.pallas_call(
        attn_fwd_kernel,
        grid=(pairs, tiles),
        in_specs=[
            pl.BlockSpec((rows, LANES), lambda p, t: (t, p)),
            pl.BlockSpec((length, LANES), lambda p, t: (0, pairs + p)),
            pl.BlockSpec((length, LANES), lambda p, t: (0, 2 * pairs + p)),
        ],
        out_specs=[
            pl.BlockSpec((rows, LANES), lambda p, t: (t, p)),
            pl.BlockSpec((1, 1, 8, rows), lambda p, t: (p, t, 0, 0)),
        ],
        out_shape=[
            jax.ShapeDtypeStruct((length, wide), BF16),
            jax.ShapeDtypeStruct((pairs, tiles, 8, rows), F32),
        ],
        compiler_params=pltpu.CompilerParams(vmem_limit_bytes=40 * 1024 * 1024),
        cost_estimate=pl.CostEstimate(
            flops=8 * length * length * wide,
            bytes_accessed=8 * length * wide,
            transcendentals=length * length * wide // HDIM,
        ),
    )(packed, packed, packed)
    return mixed[:, :columns], lse


def attention_backward(packed, d_mixed, lse):
    length = packed.shape[0]
    columns = packed.shape[1] // 3
    wide = padded_columns(columns)
    pairs = wide // LANES
    rows = query_rows(length)
    tiles = length // rows
    packed = pad_heads(packed, 3)
    d_mixed = pad_heads(d_mixed, 1)
    grads = pl.pallas_call(
        attn_bwd_kernel,
        grid=(pairs, tiles),
        in_specs=[
            pl.BlockSpec((rows, LANES), lambda p, t: (t, p)),
            pl.BlockSpec((length, LANES), lambda p, t: (0, pairs + p)),
            pl.BlockSpec((length, LANES), lambda p, t: (0, 2 * pairs + p)),
            pl.BlockSpec((rows, LANES), lambda p, t: (t, p)),
            pl.BlockSpec((1, 1, 8, rows), lambda p, t: (p, t, 0, 0)),
        ],
        out_specs=[
            pl.BlockSpec((rows, LANES), lambda p, t: (t, p)),
            pl.BlockSpec((length, LANES), lambda p, t: (0, p)),
            pl.BlockSpec((length, LANES), lambda p, t: (0, p)),
        ],
        out_shape=[jax.ShapeDtypeStruct((length, wide), BF16)] * 3,
        scratch_shapes=[pltpu.VMEM((length, LANES), F32)] * 2,
        compiler_params=pltpu.CompilerParams(vmem_limit_bytes=48 * 1024 * 1024),
        cost_estimate=pl.CostEstimate(
            flops=20 * length * length * wide,
            bytes_accessed=14 * length * wide,
            transcendentals=length * length * wide // HDIM,
        ),
    )(packed, packed, packed, d_mixed, lse)
    return jnp.concatenate([part[:, :columns] for part in grads], axis=1)


def normalized(values_in):
    centre = jnp.mean(values_in, axis=-1, keepdims=True)
    offsets = values_in - centre
    spread = jnp.mean(offsets * offsets, axis=-1, keepdims=True)
    factor = lax.rsqrt(spread + EPS)
    return offsets * factor, factor


def modulate(values_in, mod_rows, first):
    normal, _ = normalized(values_in)
    shift = mod_rows[:, first][:, None]
    scale = mod_rows[:, first + 1][:, None]
    return (normal * (1.0 + scale) + shift).astype(BF16)


def modulate_backward(values_in, d_out, mod_rows, first):
    normal, factor = normalized(values_in)
    scale = mod_rows[:, first + 1][:, None]
    d_shift = jnp.sum(d_out, axis=1)
    d_scale = jnp.sum(d_out * normal, axis=1)
    d_normal = d_out * (1.0 + scale)
    mean_plain = jnp.mean(d_normal, axis=-1, keepdims=True)
    mean_along = jnp.mean(d_normal * normal, axis=-1, keepdims=True)
    return (d_normal - mean_plain - normal * mean_along) * factor, d_shift, d_scale


def gelu_tanh(values_in):
    return jax.nn.gelu(values_in, approximate=True)


def tied(values, *others):
    return lax.optimization_barrier((values, *others))


def both(own, other):
    return jnp.concatenate([own, other], axis=0)


def rows_dot(rows, page):
    return dot32("...d,df->...f", rows, page)


def back_dot(rows, page):
    return dot32("...f,df->...d", rows, page)


def back_sum(rows_list, pages):
    return sum(back_dot(rows, page) for rows, page in zip(rows_list, pages))


def flat(values):
    return values.reshape(-1, values.shape[-1])


def row_major(values):
    return with_layout_constraint(values, Layout(major_to_minor=tuple(range(values.ndim))))


def page_grad(left, right):
    grad = lax.dot_general(
        flat(left), flat(right), (((0,), (0,)), ((), ())), preferred_element_type=F32
    )
    return row_major(grad.astype(BF16))


def token_halves(values, seqs):
    return values[:seqs], values[seqs:]


def to_attention(image_parts, text_parts):
    packed = [
        jnp.concatenate([image, text], axis=1) for image, text in zip(image_parts, text_parts)
    ]
    packed = jnp.stack(packed, axis=1)
    return packed.reshape(-1, *packed.shape[2:])


def from_attention(values, blocks, image_rows):
    values = values.reshape(-1, blocks, *values.shape[1:])
    image = [values[:, block, :image_rows] for block in range(blocks)]
    text = [values[:, block, image_rows:] for block in range(blocks)]
    return image, text


def forward_layer(streams, mods, weights, fetch):
    seqs, image_rows = streams[0].shape[:2]
    qkv_w, out_w, up_w, down_w = weights
    blocks = len(qkv_w[0])
    with jax.named_scope("attention"):
        normed = [modulate(streams[u], mods[u], 0) for u in range(2)]
        text_one = rows_of_all(normed[1])
        image_one = (normed[0], pair_swap(normed[0]))
        text_heads = rows_dot(text_one, qkv_w[1][0]).astype(BF16)
        text_heads = to_sequences(text_heads, blocks)
        image_heads = [
            both(*[rows_dot(part, page).astype(BF16) for part in image_one]) for page in qkv_w[0]
        ]
        packed = to_attention(image_heads, text_heads)
        tokens, columns = packed.shape[1:]
        next_attn = next_mlp = None
        if fetch:
            next_attn, packed = fetch[0](packed)
        packed = lax.all_to_all(packed, "dp", 0, 0, tiled=True)
        if fetch:
            next_attn, packed = attention_weights(next_attn, False, packed)
            next_mlp, packed = fetch[1](packed)
        packed = packed.reshape(-1, columns)
        mixed, lse = attention_forward(packed)
        mixed = mixed.reshape(-1, tokens, columns // 3)
        mixed = lax.all_to_all(mixed, "dp", 0, 0, tiled=True)
        if fetch:
            next_mlp, mixed = mlp_weights(next_mlp, mixed)
        image_mixed, text_mixed = from_attention(mixed, blocks, image_rows)
        text_mixed = to_blocks(text_mixed, seqs)
        other = back_sum([part[seqs:] for part in image_mixed], out_w[0])
        text_terms = back_dot(text_mixed, out_w[1][0])
        own = back_sum([part[:seqs] for part in image_mixed], out_w[0])
        attn = [pair_sum(own, other), sum_of_all(text_terms)]
    with jax.named_scope("mlp"):
        middle = [streams[u] + mods[u][:, 2][:, None] * attn[u] for u in range(2)]
        normed_two = [modulate(middle[u], mods[u], 3) for u in range(2)]
        text_two = rows_of_all(normed_two[1])
        image_two = (normed_two[0], pair_swap(normed_two[0]))
        image_up = [[rows_dot(part, page) for page in up_w[0]] for part in image_two]
        image_act = [[gelu_tanh(up).astype(BF16) for up in part] for part in image_up]
        other = back_sum(image_act[1], down_w[0])
        text_up = rows_dot(text_two, up_w[1][0])
        text_act = gelu_tanh(text_up).astype(BF16)
        text_terms = back_dot(text_act, down_w[1][0])
        own = back_sum(image_act[0], down_w[0])
        mlp = [pair_sum(own, other), sum_of_all(text_terms)]
        result = [middle[u] + mods[u][:, 5][:, None] * mlp[u] for u in range(2)]
    saved = dict(
        streams=streams,
        image_one=both(*image_one),
        text_one=text_one,
        packed=packed,
        lse=lse,
        image_mixed=image_mixed,
        text_mixed=text_mixed,
        attn=attn,
        middle=middle,
        image_two=both(*image_two),
        text_two=text_two,
        image_up=image_up,
        image_act=[both(*parts) for parts in zip(*image_act)],
        text_up=text_up,
        text_act=text_act,
        mlp=mlp,
    )
    return result, saved, (next_attn, next_mlp)


def gelu_pull(up_values, d_active):
    return jax.vjp(gelu_tanh, up_values)[1](d_active)[0].astype(BF16)


def scatter_pages(grads, after):
    wide, after = tied(jnp.concatenate(grads, axis=1), after)
    return lax.psum_scatter(wide, "dp", scatter_dimension=0, tiled=True), after


def shard_rows(slab, width, blocks):
    image = slab[:, :width].astype(F32)
    for block in range(1, blocks):
        part = slab[:, (block + 1) * width : (block + 2) * width]
        image = image + hi_swap(part, block).astype(F32)
    return image, slab[:, width : 2 * width].astype(F32)


def page_list(image_first, image_second, text_first, text_second):
    pages = [image_first[0], image_second[0], text_first, text_second]
    for pair in zip(image_first[1:], image_second[1:]):
        pages += pair
    return pages


def mlp_shard(slab, blocks):
    width = slab.shape[1] // (blocks + 1)
    rows = shard_rows(slab, width, blocks)
    half = width // 2
    return (
        jnp.stack([part[:, half:] for part in rows]),
        jnp.stack([part[:, :half].T for part in rows]),
    )


def attention_shard(slab, blocks):
    width = slab.shape[1] // (blocks + 1)
    rows = shard_rows(slab, width, blocks)
    columns = width // 4
    return (
        jnp.stack(
            [
                part[:, : 3 * columns].reshape(-1, 3, columns).transpose(1, 0, 2)
                for part in rows
            ]
        ),
        jnp.stack([part[:, 3 * columns :].T for part in rows]),
    )


def backward_layer(grads_out, mods, weights, saved, pending):
    seqs, image_rows = grads_out[0].shape[:2]
    qkv_w, out_w, up_w, down_w = weights
    blocks = len(qkv_w[0])
    middle, attn, mlp = saved["middle"], saved["attn"], saved["mlp"]
    with jax.named_scope("mlp_grad"):
        gated = [(mods[u][:, 5][:, None] * grads_out[u]).astype(BF16) for u in range(2)]
        text_dmlp = rows_of_all(gated[1])
        image_dmlp = (gated[0], pair_swap(gated[0]))
        d_gate_two = [jnp.sum(grads_out[u] * mlp[u], axis=1) for u in range(2)]
        image_dup = [
            [
                gelu_pull(saved["image_up"][at][block], rows_dot(image_dmlp[at], down_w[0][block]))
                for block in range(blocks)
            ]
            for at in range(2)
        ]
        other = back_sum(image_dup[1], up_w[0])
        text_dup = gelu_pull(saved["text_up"], rows_dot(text_dmlp, down_w[1][0]))
        text_terms = back_dot(text_dup, up_w[1][0])
        own = back_sum(image_dup[0], up_w[0])
        dmlp_rows = both(*image_dmlp)
        received = pair_swap(other.astype(BF16))
        grads = page_list(
            [page_grad(dmlp_rows, act) for act in saved["image_act"]],
            [page_grad(saved["image_two"], both(*parts)) for parts in zip(*image_dup)],
            page_grad(text_dmlp, saved["text_act"]),
            page_grad(saved["text_two"], text_dup),
        )
        mlp_slab, received = scatter_pages(grads, received)
        d_two = [own + received.astype(F32), sum_of_all(text_terms)]
        d_middle, d_shift_two, d_scale_two = [], [], []
        for u in range(2):
            d_values, d_shift, d_scale = modulate_backward(middle[u], d_two[u], mods[u], 3)
            d_middle.append(grads_out[u] + d_values)
            d_shift_two.append(d_shift)
            d_scale_two.append(d_scale)
    with jax.named_scope("attention_grad"):
        gated = [(mods[u][:, 2][:, None] * d_middle[u]).astype(BF16) for u in range(2)]
        text_dattn = rows_of_all(gated[1])
        image_dattn = (gated[0], pair_swap(gated[0]))
        d_gate_one = [jnp.sum(d_middle[u] * attn[u], axis=1) for u in range(2)]
        text_dmixed = to_sequences(rows_dot(text_dattn, out_w[1][0]).astype(BF16), blocks)
        image_dmixed = [
            both(*[rows_dot(part, page).astype(BF16) for part in image_dattn]) for page in out_w[0]
        ]
        d_mixed = to_attention(image_dmixed, text_dmixed)
        tokens, columns = d_mixed.shape[1:]
        d_mixed = lax.all_to_all(d_mixed, "dp", 0, 0, tiled=True)
        done = []
        if pending:
            mlp_before, d_mixed = tied(pending[0], d_mixed)
            done.append(mlp_shard(mlp_before, blocks))
        d_mixed = d_mixed.reshape(-1, columns)
        d_packed = attention_backward(saved["packed"], d_mixed, saved["lse"])
        d_packed = d_packed.reshape(-1, tokens, 3 * columns)
        d_packed = lax.all_to_all(d_packed, "dp", 0, 0, tiled=True)
        if pending:
            done[0], attn_before, d_packed = tied(done[0], pending[1], d_packed)
            done.append(attention_shard(attn_before, blocks))
        image_dproj, text_dproj = from_attention(d_packed, blocks, image_rows)
        text_dproj = to_blocks(text_dproj, seqs)
        other = back_sum([part[seqs:] for part in image_dproj], qkv_w[0])
        received = pair_swap(other.astype(BF16))
        text_terms = back_dot(text_dproj, qkv_w[1][0])
        own = back_sum([part[:seqs] for part in image_dproj], qkv_w[0])
        dattn_rows = both(*image_dattn)
        grads = page_list(
            [page_grad(saved["image_one"], part) for part in image_dproj],
            [page_grad(dattn_rows, part) for part in saved["image_mixed"]],
            page_grad(saved["text_one"], text_dproj),
            page_grad(text_dattn, saved["text_mixed"]),
        )
        attn_slab, (mlp_slab, done) = scatter_pages(grads, (mlp_slab, done))
        d_one = [own + received.astype(F32), sum_of_all(text_terms)]
        d_inputs, d_mods = [], []
        for u in range(2):
            d_values, d_shift, d_scale = modulate_backward(
                saved["streams"][u], d_one[u], mods[u], 0
            )
            d_inputs.append(d_middle[u] + d_values)
            d_mods.append(
                jnp.stack(
                    [d_shift, d_scale, d_gate_one[u], d_shift_two[u], d_scale_two[u], d_gate_two[u]],
                    axis=1,
                )
            )
    return d_inputs, jnp.stack(d_mods), (mlp_slab, attn_slab), done


def with_blocks(pages):
    hi_count = lax.axis_size("tensor") // 2
    return [pages] + [hi_swap(pages, block) for block in range(1, hi_count)]


def gather_pages(pages):
    return lax.all_gather(pages, "dp", axis=1, tiled=True)


def attn_page(w_qkv, w_out, layer_at, u):
    qkv = w_qkv[layer_at, u].transpose(1, 0, 2)
    qkv = qkv.reshape(qkv.shape[0], -1)
    return jnp.concatenate([qkv, w_out[layer_at, u].T], axis=1)


def attention_shards(w_qkv, w_out, layer_at, after):
    own = [attn_page(w_qkv, w_out, layer_at, u)[None] for u in range(2)]
    own, after = tied(own, after)
    lists = with_blocks(own[0])
    return [lists[0], own[1], *lists[1:]], after


def attention_weights(lists, split, after):
    lists, after = tied(lists, after)
    if split:
        first = gather_pages(jnp.concatenate(lists[:2], axis=0))
        rest, first = tied(lists[2:], first)
        rest = gather_pages(jnp.concatenate(rest, axis=0))
        pages = [first[0], first[1]] + [rest[at] for at in range(len(lists) - 2)]
    else:
        whole = gather_pages(jnp.concatenate(lists, axis=0))
        pages = [whole[at] for at in range(len(lists))]
    qkv_columns = lists[0].shape[2] * 3 // 4
    by_stream = [[pages[0], *pages[2:]], [pages[1]]]
    qkv_w = [[page[:, :qkv_columns] for page in group] for group in by_stream]
    out_w = [[page[:, qkv_columns:] for page in group] for group in by_stream]
    return (qkv_w, out_w), after


def mlp_shards(w_up, w_down, layer_at, after):
    own = [jnp.stack([w_up[layer_at, u], w_down[layer_at, u].T]) for u in range(2)]
    own, after = tied(own, after)
    return with_blocks(own[0]) + [own[1]], after


def mlp_weights(lists, after):
    lists, after = tied(lists, after)
    blocks = len(lists) - 1
    whole = gather_pages(jnp.concatenate(lists, axis=0))
    up_w = [[whole[2 * at] for at in range(blocks)], [whole[2 * blocks]]]
    down_w = [[whole[2 * at + 1] for at in range(blocks)], [whole[2 * blocks + 1]]]
    return (up_w, down_w), after


def per_device(
    image_in,
    text_in,
    cond_table,
    cond_index,
    w_mod,
    w_qkv,
    w_out,
    w_up,
    w_down,
    cot_image,
    cot_text,
):
    n_tensor = lax.axis_size("tensor")
    dp_at = lax.axis_index("dp")
    micro_count, own_rows = image_in.shape[:2]
    seqs = micro_count * own_rows
    model_width = image_in.shape[3]
    layer_count = w_qkv.shape[0]
    slab_rows = w_mod.shape[2]
    column_count = w_mod.shape[3]
    index_flat = cond_index.reshape(-1)
    attn_w, _ = attention_weights(attention_shards(w_qkv, w_out, 0, ())[0], True, ())
    mlp_lists, _ = mlp_shards(w_up, w_down, 0, ())
    with jax.named_scope("modulation"):
        onehot = (
            index_flat[:, None] == jnp.arange(cond_table.shape[0], dtype=jnp.int32)[None, :]
        ).astype(F32)
        cond_slab = lax.dynamic_slice_in_dim(cond_table, dp_at * slab_rows, slab_rows, 1)
        cond_slab = jnp.dot(onehot, cond_slab, precision=HIGHEST, preferred_element_type=F32)
        silu_slab = jax.nn.silu(cond_slab).astype(BF16)
        partial_mod = dot32("sd,lmdc->lmsc", silu_slab, w_mod)
        partial_mod = partial_mod.reshape(
            layer_count * 2, micro_count, n_tensor, own_rows * column_count
        )
        partial_mod = partial_mod.transpose(2, 0, 1, 3).reshape(n_tensor, -1, column_count)
        partial_mod = dp_sum(lax.all_to_all(partial_mod, "tensor", 0, 0, tiled=True))
        mod_own = partial_mod.transpose(1, 0, 2)
        mod_own = mod_own.reshape(layer_count, 2, seqs, 6, model_width)
    mlp_w, mod_own = mlp_weights(mlp_lists, mod_own)
    mods = [[mod_own[layer_at, u] for u in range(2)] for layer_at in range(layer_count)]

    def rows_in(values):
        return values.reshape(seqs, values.shape[2], model_width).astype(F32)

    def rows_out(values):
        return values.reshape(micro_count, own_rows, values.shape[1], model_width)

    streams = [rows_in(image_in), rows_in(text_in)]
    saved, weights = [], []
    for layer_at in range(layer_count):
        weights.append((*attn_w, *mlp_w))
        fetch = None
        if layer_at + 1 < layer_count:
            fetch = (
                functools.partial(attention_shards, w_qkv, w_out, layer_at + 1),
                functools.partial(mlp_shards, w_up, w_down, layer_at + 1),
            )
        streams, kept, (attn_w, mlp_w) = forward_layer(
            streams, mods[layer_at], weights[layer_at], fetch
        )
        saved.append(kept)
    grads_now = [rows_in(cot_image), rows_in(cot_text)]
    shards = [None] * layer_count
    d_cond_terms = []
    grad_w_mod = [None] * layer_count
    pending = None
    for layer_at in reversed(range(layer_count)):
        grads_now, d_mods, slabs, done = backward_layer(
            grads_now, mods[layer_at], weights[layer_at], saved[layer_at], pending
        )
        if pending:
            shards[layer_at + 1] = done
        pending = slabs
        with jax.named_scope("modulation_grad"):
            d_mods = d_mods.reshape(2 * seqs, n_tensor, column_count).transpose(1, 0, 2)
            d_mods = dp_sum(lax.all_to_all(d_mods, "tensor", 0, 0, tiled=True))
            d_mods = d_mods.reshape(n_tensor, 2, micro_count, own_rows, column_count)
            d_mods = d_mods.transpose(1, 2, 0, 3, 4)
            d_columns = d_mods.reshape(2, micro_count * n_tensor * own_rows, column_count)
            grad_w_mod[layer_at] = jnp.einsum(
                "sd,msc->mdc",
                silu_slab.astype(F32),
                d_columns,
                precision=HIGHEST,
                preferred_element_type=F32,
            )
            d_cond_terms.append(
                jnp.einsum(
                    "msc,mdc->sd",
                    d_columns,
                    w_mod[layer_at].astype(F32),
                    precision=HIGHEST,
                    preferred_element_type=F32,
                )
            )
    with jax.named_scope("conditioning_grad"):
        d_silu = sum(d_cond_terms)
        d_cond = jax.vjp(jax.nn.silu, cond_slab)[1](d_silu)[0]
        grad_cond = lax.psum(
            jnp.dot(onehot.T, d_cond, precision=HIGHEST, preferred_element_type=F32), "tensor"
        )
    with jax.named_scope("weight_grads"):
        blocks = n_tensor // 2
        shards[0] = (mlp_shard(pending[0], blocks), attention_shard(pending[1], blocks))
        stacked = [
            jnp.stack([layer[part][at] for layer in shards])
            for part, at in ((1, 0), (1, 1), (0, 0), (0, 1))
        ]
    return (
        rows_out(streams[0].astype(BF16)),
        rows_out(streams[1].astype(BF16)),
        rows_out(grads_now[0]),
        rows_out(grads_now[1]),
        grad_cond,
        jnp.stack(grad_w_mod),
        *stacked,
    )


def solution(mesh):
    rows = P(None, "tensor", "dp", None)
    up_like = P(None, None, "dp", "tensor")
    down_like = P(None, None, "tensor", "dp")
    qkv_like = P(None, None, None, "dp", "tensor")
    return jax.shard_map(
        per_device,
        mesh=mesh,
        in_specs=(
            rows,
            rows,
            P(),
            P(),
            up_like,
            qkv_like,
            down_like,
            up_like,
            down_like,
            rows,
            rows,
        ),
        out_specs=(
            rows,
            rows,
            rows,
            rows,
            P(None, "dp"),
            up_like,
            qkv_like,
            down_like,
            up_like,
            down_like,
        ),
        check_vma=False,
    )
```

```python
import functools

import jax
import jax.numpy as jnp
from jax import lax
from jax.experimental import pallas as pl
from jax.experimental.layout import Layout, with_layout_constraint
from jax.experimental.pallas import tpu as pltpu
from jax.sharding import PartitionSpec as P

HDIM = 64
LANES = 128
EPS = 1e-06
HIGHEST = lax.Precision.HIGHEST
BF16 = jnp.bfloat16
F32 = jnp.float32


def dot32(pattern, left, right):
    return jnp.einsum(pattern, left, right, preferred_element_type=F32)


def tensor_swap(values, distance):
    count = lax.axis_size("tensor")
    return lax.ppermute(values, "tensor", [(i, i ^ distance) for i in range(count)])


def pair_swap(values):
    return tensor_swap(values, 1)


def hi_swap(values, block):
    return tensor_swap(values, 2 * block)


def axis_sum(values, axis):
    count = lax.axis_size(axis)
    step = 1
    while step < count:
        values = values + lax.ppermute(values, axis, [(i, i ^ step) for i in range(count)])
        step *= 2
    return values


def rows_of_others(image, text):
    image_rows = image.shape[1]
    received = pair_swap(jnp.concatenate([image, text], axis=1))
    far = [tensor_swap(text, at) for at in range(2, lax.axis_size("tensor"))]
    return (image, received[:, :image_rows]), jnp.stack([text, received[:, image_rows:], *far])


def sum_over_others(image_own, image_other, text_terms, *meanwhile):
    image_rows = image_own.shape[1]
    sent = jnp.concatenate([image_other.astype(BF16), text_terms[1].astype(BF16)], axis=1)
    received = pair_swap(sent)
    far = [
        tensor_swap(text_terms[at].astype(BF16), at) for at in range(2, text_terms.shape[0])
    ]
    received, far, *meanwhile = tied(received, far, *meanwhile)
    image = image_own + received[:, :image_rows].astype(F32)
    text = text_terms[0] + received[:, image_rows:].astype(F32)
    for part in far:
        text = text + part.astype(F32)
    return [image, text], *meanwhile


def to_sequences(parts, blocks):
    received = [parts[:2]] + [
        hi_swap(parts[2 * block : 2 * block + 2], block) for block in range(1, blocks)
    ]
    return [flat_pairs(part) for part in received]


def to_blocks(by_block, seqs):
    split = [part.reshape(2, seqs, *part.shape[1:]) for part in by_block]
    parts = [split[0]] + [hi_swap(split[block], block) for block in range(1, len(split))]
    return jnp.concatenate(parts, axis=0)


def flat_pairs(values):
    return values.reshape(-1, *values.shape[2:])


def head_mask(rows, which):
    lane = lax.broadcasted_iota(jnp.int32, (rows, LANES), 1)
    return (lane < HDIM) if which == 0 else (lane >= HDIM)


def nt_dot(left, right):
    return lax.dot_general(left, right, (((1,), (1,)), ((), ())), preferred_element_type=F32)


def attn_fwd_kernel(q_ref, k_ref, v_ref, o_ref, lse_ref):
    rows = q_ref.shape[0]
    queries = q_ref[...] * jnp.asarray(HDIM ** (-0.5), BF16)
    keys = k_ref[...]
    values_t = v_ref[...].astype(F32).T.astype(BF16)
    parts = []
    for which in range(2):
        masked = jnp.where(head_mask(rows, which), queries, jnp.zeros_like(queries))
        scores = nt_dot(keys, masked)
        peak = jnp.max(scores, axis=0, keepdims=True)
        raised = jnp.exp(scores - peak)
        total = jnp.sum(raised, axis=0, keepdims=True)
        out_t = jnp.dot(
            values_t[which * HDIM : (which + 1) * HDIM],
            raised.astype(BF16),
            preferred_element_type=F32,
        )
        parts.append(out_t * (1.0 / total))
        lse_ref[0, 0, which : which + 1, :] = peak + jnp.log(total)
    o_ref[...] = jnp.concatenate(parts, axis=0).T.astype(BF16)


def attn_bwd_kernel(q_ref, k_ref, v_ref, do_ref, lse_ref, dq_ref, dk_ref, dv_ref, dk_acc, dv_acc):
    tile = pl.program_id(1)
    rows = q_ref.shape[0]
    scale = HDIM ** (-0.5)

    @pl.when(tile == 0)
    def _():
        dk_acc[...] = jnp.zeros_like(dk_acc)
        dv_acc[...] = jnp.zeros_like(dv_acc)

    queries = q_ref[...] * jnp.asarray(scale, BF16)
    d_out = do_ref[...]
    keys = k_ref[...]
    values = v_ref[...]
    keys_t = keys.astype(F32).T.astype(BF16)
    parts = []
    for which in range(2):
        mask = head_mask(rows, which)
        q_masked = jnp.where(mask, queries, jnp.zeros_like(queries))
        do_masked = jnp.where(mask, d_out, jnp.zeros_like(d_out))
        scores = nt_dot(keys, q_masked)
        probs = jnp.exp(scores - lse_ref[0, 0, which : which + 1, :])
        d_probs = nt_dot(values, do_masked)
        centre = jnp.sum(probs * d_probs, axis=0, keepdims=True)
        d_scores = (probs * (d_probs - centre)).astype(BF16)
        dv_acc[...] += jnp.dot(probs.astype(BF16), do_masked, preferred_element_type=F32)
        dk_acc[...] += jnp.dot(d_scores, q_masked, preferred_element_type=F32)
        parts.append(
            jnp.dot(
                keys_t[which * HDIM : (which + 1) * HDIM], d_scores, preferred_element_type=F32
            )
        )
    dq_ref[...] = (jnp.concatenate(parts, axis=0).T * scale).astype(BF16)

    @pl.when(tile == pl.num_programs(1) - 1)
    def _():
        dk_ref[...] = dk_acc[...].astype(BF16)
        dv_ref[...] = dv_acc[...].astype(BF16)


def query_rows(length):
    return length // 2 if length % 32 == 0 else length


def padded_columns(columns):
    return -(-columns // LANES) * LANES


def pad_heads(packed, pieces):
    columns = packed.shape[1] // pieces
    wide = padded_columns(columns)
    if wide == columns:
        return packed
    split = packed.reshape(packed.shape[0], pieces, columns)
    return jnp.pad(split, ((0, 0), (0, 0), (0, wide - columns))).reshape(
        packed.shape[0], pieces * wide
    )


def attention_forward(packed):
    length = packed.shape[0]
    columns = packed.shape[1] // 3
    wide = padded_columns(columns)
    pairs = wide // LANES
    rows = query_rows(length)
    tiles = length // rows
    packed = pad_heads(packed, 3)
    mixed, lse = pl.pallas_call(
        attn_fwd_kernel,
        grid=(pairs, tiles),
        in_specs=[
            pl.BlockSpec((rows, LANES), lambda p, t: (t, p)),
            pl.BlockSpec((length, LANES), lambda p, t: (0, pairs + p)),
            pl.BlockSpec((length, LANES), lambda p, t: (0, 2 * pairs + p)),
        ],
        out_specs=[
            pl.BlockSpec((rows, LANES), lambda p, t: (t, p)),
            pl.BlockSpec((1, 1, 8, rows), lambda p, t: (p, t, 0, 0)),
        ],
        out_shape=[
            jax.ShapeDtypeStruct((length, wide), BF16),
            jax.ShapeDtypeStruct((pairs, tiles, 8, rows), F32),
        ],
        compiler_params=pltpu.CompilerParams(vmem_limit_bytes=40 * 1024 * 1024),
        cost_estimate=pl.CostEstimate(
            flops=8 * length * length * wide,
            bytes_accessed=8 * length * wide,
            transcendentals=length * length * wide // HDIM,
        ),
    )(packed, packed, packed)
    return mixed[:, :columns], lse


def attention_backward(packed, d_mixed, lse):
    length = packed.shape[0]
    columns = packed.shape[1] // 3
    wide = padded_columns(columns)
    pairs = wide // LANES
    rows = query_rows(length)
    tiles = length // rows
    packed = pad_heads(packed, 3)
    d_mixed = pad_heads(d_mixed, 1)
    grads = pl.pallas_call(
        attn_bwd_kernel,
        grid=(pairs, tiles),
        in_specs=[
            pl.BlockSpec((rows, LANES), lambda p, t: (t, p)),
            pl.BlockSpec((length, LANES), lambda p, t: (0, pairs + p)),
            pl.BlockSpec((length, LANES), lambda p, t: (0, 2 * pairs + p)),
            pl.BlockSpec((rows, LANES), lambda p, t: (t, p)),
            pl.BlockSpec((1, 1, 8, rows), lambda p, t: (p, t, 0, 0)),
        ],
        out_specs=[
            pl.BlockSpec((rows, LANES), lambda p, t: (t, p)),
            pl.BlockSpec((length, LANES), lambda p, t: (0, p)),
            pl.BlockSpec((length, LANES), lambda p, t: (0, p)),
        ],
        out_shape=[jax.ShapeDtypeStruct((length, wide), BF16)] * 3,
        scratch_shapes=[pltpu.VMEM((length, LANES), F32)] * 2,
        compiler_params=pltpu.CompilerParams(vmem_limit_bytes=48 * 1024 * 1024),
        cost_estimate=pl.CostEstimate(
            flops=20 * length * length * wide,
            bytes_accessed=14 * length * wide,
            transcendentals=length * length * wide // HDIM,
        ),
    )(packed, packed, packed, d_mixed, lse)
    return jnp.concatenate([part[:, :columns] for part in grads], axis=1)


def normalized(values_in):
    centre = jnp.mean(values_in, axis=-1, keepdims=True)
    offsets = values_in - centre
    spread = jnp.mean(offsets * offsets, axis=-1, keepdims=True)
    factor = lax.rsqrt(spread + EPS)
    return offsets * factor, factor


def modulate(values_in, mod_rows, first):
    normal, _ = normalized(values_in)
    shift = mod_rows[:, first][:, None]
    scale = mod_rows[:, first + 1][:, None]
    return (normal * (1.0 + scale) + shift).astype(BF16)


def modulate_backward(values_in, d_out, mod_rows, first):
    normal, factor = normalized(values_in)
    scale = mod_rows[:, first + 1][:, None]
    d_shift = jnp.sum(d_out, axis=1)
    d_scale = jnp.sum(d_out * normal, axis=1)
    d_normal = d_out * (1.0 + scale)
    mean_plain = jnp.mean(d_normal, axis=-1, keepdims=True)
    mean_along = jnp.mean(d_normal * normal, axis=-1, keepdims=True)
    return (d_normal - mean_plain - normal * mean_along) * factor, d_shift, d_scale


def gelu_tanh(values_in):
    return jax.nn.gelu(values_in, approximate=True)


def tied(values, *others):
    return lax.optimization_barrier((values, *others))


def both(own, other):
    return jnp.concatenate([own, other], axis=0)


def rows_dot(rows, page):
    return dot32("...d,df->...f", rows, page)


def back_dot(rows, page):
    return dot32("...f,df->...d", rows, page)


def back_sum(rows_list, pages):
    return sum(back_dot(rows, page) for rows, page in zip(rows_list, pages))


def flat(values):
    return values.reshape(-1, values.shape[-1])


def row_major(values):
    return with_layout_constraint(values, Layout(major_to_minor=tuple(range(values.ndim))))


def page_grad(left, right):
    grad = lax.dot_general(
        flat(left), flat(right), (((0,), (0,)), ((), ())), preferred_element_type=F32
    )
    return row_major(grad.astype(BF16))


def token_halves(values, seqs):
    return values[:seqs], values[seqs:]


def to_attention(image_parts, text_parts):
    packed = [
        jnp.concatenate([image, text], axis=1) for image, text in zip(image_parts, text_parts)
    ]
    packed = jnp.stack(packed, axis=1)
    return packed.reshape(-1, *packed.shape[2:])


def from_attention(values, blocks, image_rows):
    values = values.reshape(-1, blocks, *values.shape[1:])
    image = [values[:, block, :image_rows] for block in range(blocks)]
    text = [values[:, block, image_rows:] for block in range(blocks)]
    return image, text


def forward_layer(streams, mods, attn_w, mlp_shards, next_shards):
    seqs, image_rows = streams[0].shape[:2]
    with jax.named_scope("attention"):
        normed = [modulate(streams[u], mods[u], 0) for u in range(2)]
        image_one, text_one = rows_of_others(*normed)
        text_one, attn_w, mlp_shards, next_shards = tied(
            text_one, attn_w, mlp_shards, next_shards
        )
        mlp_w = [gather_pages(jnp.concatenate(mlp_shards, axis=0))]
        mlp_others = with_blocks(mlp_shards[0])[1:]
        next_others = with_blocks(next_shards[0])[1:] if next_shards else []
        qkv_w, out_w = attention_pages(attn_w)
        blocks = len(qkv_w[0])
        text_heads = rows_dot(text_one, qkv_w[1][0]).astype(BF16)
        text_heads = to_sequences(text_heads, blocks)
        image_heads = [
            both(*[rows_dot(part, page).astype(BF16) for part in image_one]) for page in qkv_w[0]
        ]
        packed = to_attention(image_heads, text_heads)
        tokens, columns = packed.shape[1:]
        packed = lax.all_to_all(packed, "dp", 0, 0, tiled=True)
        packed = packed.reshape(-1, columns)
        mixed, lse = attention_forward(packed)
        mixed = mixed.reshape(-1, tokens, columns // 3)
        mixed = lax.all_to_all(mixed, "dp", 0, 0, tiled=True)
        mixed, mlp_others, next_others = tied(mixed, mlp_others, next_others)
        mlp_others, mlp_w[0] = tied(mlp_others, mlp_w[0])
        mlp_w.append(gather_pages(jnp.concatenate(mlp_others, axis=0)))
        image_mixed, text_mixed = from_attention(mixed, blocks, image_rows)
        text_mixed = to_blocks(text_mixed, seqs)
        other = back_sum([part[seqs:] for part in image_mixed], out_w[0])
        text_terms = back_dot(text_mixed, out_w[1][0])
        own = back_sum([part[:seqs] for part in image_mixed], out_w[0])
        (attn,) = sum_over_others(own, other, text_terms)
    with jax.named_scope("mlp"):
        middle = [streams[u] + mods[u][:, 2][:, None] * attn[u] for u in range(2)]
        normed_two = [modulate(middle[u], mods[u], 3) for u in range(2)]
        image_two, text_two = rows_of_others(*normed_two)
        text_two, mlp_w, next_shards, next_others = tied(
            text_two, mlp_w, next_shards, next_others
        )
        next_attn = None
        if next_shards:
            next_attn = (gather_pages(jnp.concatenate([*next_shards, *next_others], axis=0)),)
        up_w, down_w = mlp_pages(mlp_w)
        image_up = [[rows_dot(part, page) for page in up_w[0]] for part in image_two]
        image_act = [[gelu_tanh(up).astype(BF16) for up in part] for part in image_up]
        other = back_sum(image_act[1], down_w[0]).astype(BF16)
        text_up = rows_dot(text_two, up_w[1][0])
        text_act = gelu_tanh(text_up).astype(BF16)
        text_terms = back_dot(text_act, down_w[1][0])
        own = back_sum(image_act[0], down_w[0])
        (mlp,) = sum_over_others(own, other, text_terms)
        result = [middle[u] + mods[u][:, 5][:, None] * mlp[u] for u in range(2)]
    saved = dict(
        streams=streams,
        image_one=both(*image_one),
        text_one=text_one,
        packed=packed,
        lse=lse,
        image_mixed=image_mixed,
        text_mixed=text_mixed,
        attn=attn,
        middle=middle,
        image_two=both(*image_two),
        text_two=text_two,
        image_up=image_up,
        image_act=[both(*parts) for parts in zip(*image_act)],
        text_up=text_up,
        text_act=text_act,
        mlp=mlp,
    )
    return result, saved, (attn_w, mlp_w), next_attn


def gelu_pull(up_values, d_active):
    return jax.vjp(gelu_tanh, up_values)[1](d_active)[0].astype(BF16)


def scatter_pages(wide):
    return lax.psum_scatter(wide, "dp", scatter_dimension=0, tiled=True)


def shard_rows(slab, width, blocks):
    image = slab[:, :width].astype(F32)
    for block in range(1, blocks):
        part = slab[:, (block + 1) * width : (block + 2) * width]
        image = image + hi_swap(part, block).astype(F32)
    return image, slab[:, width : 2 * width].astype(F32)


def page_list(image_first, image_second, text_first, text_second):
    pages = [image_first[0], image_second[0], text_first, text_second]
    for pair in zip(image_first[1:], image_second[1:]):
        pages += pair
    return pages


def mlp_shard(slab, blocks):
    width = slab.shape[1] // (blocks + 1)
    rows = shard_rows(slab, width, blocks)
    half = width // 2
    return (
        jnp.stack([part[:, half:] for part in rows]),
        jnp.stack([part[:, :half].T for part in rows]),
    )


def attention_shard(slab, blocks):
    width = slab.shape[1] // (blocks + 1)
    rows = shard_rows(slab, width, blocks)
    columns = width // 4
    return (
        jnp.stack(
            [
                jnp.stack([part[:, at * columns : (at + 1) * columns] for at in range(3)])
                for part in rows
            ]
        ),
        jnp.stack([part[:, 3 * columns :].T for part in rows]),
    )


def backward_layer(grads_out, mods, weights, saved, pending, final):
    seqs, image_rows = grads_out[0].shape[:2]
    qkv_w, out_w = attention_pages(weights[0])
    up_w, down_w = mlp_pages(weights[1])
    blocks = len(qkv_w[0])
    middle, attn, mlp = saved["middle"], saved["attn"], saved["mlp"]
    with jax.named_scope("mlp_grad"):
        gated = [(mods[u][:, 5][:, None] * grads_out[u]).astype(BF16) for u in range(2)]
        image_dmlp, text_dmlp = rows_of_others(*gated)
        d_gate_two = [jnp.sum(grads_out[u] * mlp[u], axis=1) for u in range(2)]
        image_dup = [
            [
                gelu_pull(saved["image_up"][at][block], rows_dot(image_dmlp[at], down_w[0][block]))
                for block in range(blocks)
            ]
            for at in range(2)
        ]
        other = back_sum(image_dup[1], up_w[0])
        text_dup = gelu_pull(saved["text_up"], rows_dot(text_dmlp, down_w[1][0]))
        text_terms = back_dot(text_dup, up_w[1][0])
        own = back_sum(image_dup[0], up_w[0])
        dmlp_rows = both(*image_dmlp)
        grads = page_list(
            [page_grad(dmlp_rows, act) for act in saved["image_act"]],
            [page_grad(saved["image_two"], both(*parts)) for parts in zip(*image_dup)],
            page_grad(text_dmlp, saved["text_act"]),
            page_grad(saved["text_two"], text_dup),
        )
        wide = jnp.concatenate(grads, axis=1)
        d_two, wide = sum_over_others(own, other, text_terms, wide)
        mlp_slab = scatter_pages(wide)
        d_middle, d_shift_two, d_scale_two = [], [], []
        for u in range(2):
            d_values, d_shift, d_scale = modulate_backward(middle[u], d_two[u], mods[u], 3)
            d_middle.append(grads_out[u] + d_values)
            d_shift_two.append(d_shift)
            d_scale_two.append(d_scale)
    with jax.named_scope("attention_grad"):
        gated = [(mods[u][:, 2][:, None] * d_middle[u]).astype(BF16) for u in range(2)]
        image_dattn, text_dattn = rows_of_others(*gated)
        d_gate_one = [jnp.sum(d_middle[u] * attn[u], axis=1) for u in range(2)]
        text_dmixed = to_sequences(rows_dot(text_dattn, out_w[1][0]).astype(BF16), blocks)
        image_dmixed = [
            both(*[rows_dot(part, page).astype(BF16) for part in image_dattn]) for page in out_w[0]
        ]
        d_mixed = to_attention(image_dmixed, text_dmixed)
        tokens, columns = d_mixed.shape[1:]
        d_mixed = lax.all_to_all(d_mixed, "dp", 0, 0, tiled=True)
        done = []
        if pending:
            mlp_before, d_mixed = tied(pending[0], d_mixed)
            done.append(mlp_shard(mlp_before, blocks))
        d_mixed = d_mixed.reshape(-1, columns)
        d_packed = attention_backward(saved["packed"], d_mixed, saved["lse"])
        d_packed = d_packed.reshape(-1, tokens, 3 * columns)
        d_packed = lax.all_to_all(d_packed, "dp", 0, 0, tiled=True)
        if pending:
            done[0], attn_before, d_packed = tied(done[0], pending[1], d_packed)
            done.append(attention_shard(attn_before, blocks))
        image_dproj, text_dproj = from_attention(d_packed, blocks, image_rows)
        text_dproj = to_blocks(text_dproj, seqs)
        grad_rows = image_dproj
        if not final:
            other = back_sum([part[seqs:] for part in image_dproj], qkv_w[0]).astype(BF16)
            grad_rows, other = tied(image_dproj, other)
        dattn_rows = both(*image_dattn)
        grads = page_list(
            [page_grad(saved["image_one"], part) for part in grad_rows],
            [page_grad(dattn_rows, part) for part in saved["image_mixed"]],
            page_grad(saved["text_one"], text_dproj),
            page_grad(text_dattn, saved["text_mixed"]),
        )
        wide = jnp.concatenate(grads, axis=1)
        if final:
            wide, image_dproj = tied(wide, image_dproj)
            other = back_sum([part[seqs:] for part in image_dproj], qkv_w[0]).astype(BF16)
        text_terms = back_dot(text_dproj, qkv_w[1][0])
        own = back_sum([part[:seqs] for part in image_dproj], qkv_w[0])
        (d_one,) = sum_over_others(own, other, text_terms)
        wide, mlp_slab = tied(wide, mlp_slab)
        attn_slab = scatter_pages(wide)
        d_inputs, d_mods = [], []
        for u in range(2):
            d_values, d_shift, d_scale = modulate_backward(
                saved["streams"][u], d_one[u], mods[u], 0
            )
            d_inputs.append(d_middle[u] + d_values)
            d_mods.append(
                jnp.concatenate(
                    [d_shift, d_scale, d_gate_one[u], d_shift_two[u], d_scale_two[u], d_gate_two[u]],
                    axis=1,
                )
            )
    return d_inputs, jnp.concatenate(d_mods), (mlp_slab, attn_slab), done


def with_blocks(pages):
    hi_count = lax.axis_size("tensor") // 2
    return [pages] + [hi_swap(pages, block) for block in range(1, hi_count)]


def gather_pages(pages):
    return lax.all_gather(pages, "dp", axis=1, tiled=True)


def attn_page(w_qkv, w_out, layer_at, u):
    qkv = w_qkv[layer_at, u].transpose(1, 0, 2)
    qkv = qkv.reshape(qkv.shape[0], -1)
    return jnp.concatenate([qkv, w_out[layer_at, u].T], axis=1)


def attention_shards(w_qkv, w_out, layer_at):
    return [attn_page(w_qkv, w_out, layer_at, u)[None] for u in range(2)]


def mlp_shards(w_up, w_down, layer_at):
    return [jnp.stack([w_up[layer_at, u], w_down[layer_at, u].T]) for u in range(2)]


def attention_pages(gathered):
    pages = [pages[at] for pages in gathered for at in range(pages.shape[0])]
    qkv_columns = pages[0].shape[1] * 3 // 4
    by_stream = [[pages[0], *pages[2:]], [pages[1]]]
    qkv_w = [[page[:, :qkv_columns] for page in group] for group in by_stream]
    out_w = [[page[:, qkv_columns:] for page in group] for group in by_stream]
    return qkv_w, out_w


def mlp_pages(gathered):
    pages = [pages[at] for pages in gathered for at in range(pages.shape[0])]
    by_stream = [[*pages[:2], *pages[4:]], pages[2:4]]
    return [group[0::2] for group in by_stream], [group[1::2] for group in by_stream]


def per_device(
    image_in,
    text_in,
    cond_table,
    cond_index,
    w_mod,
    w_qkv,
    w_out,
    w_up,
    w_down,
    cot_image,
    cot_text,
):
    n_tensor = lax.axis_size("tensor")
    dp_at = lax.axis_index("dp")
    micro_count, own_rows = image_in.shape[:2]
    seqs = micro_count * own_rows
    model_width = image_in.shape[3]
    layer_count = w_qkv.shape[0]
    slab_rows = w_mod.shape[2]
    column_count = w_mod.shape[3]
    index_flat = cond_index.reshape(-1)
    attn_shards = [attention_shards(w_qkv, w_out, at) for at in range(layer_count)]
    all_mlp_shards = [mlp_shards(w_up, w_down, at) for at in range(layer_count)]
    first_attn = gather_pages(jnp.concatenate(attn_shards[0], axis=0))
    with jax.named_scope("modulation"):
        onehot = (
            index_flat[:, None] == jnp.arange(cond_table.shape[0], dtype=jnp.int32)[None, :]
        ).astype(F32)
        cond_slab = lax.dynamic_slice_in_dim(cond_table, dp_at * slab_rows, slab_rows, 1)
        cond_slab = jnp.dot(onehot, cond_slab, precision=HIGHEST, preferred_element_type=F32)
        silu_slab = jax.nn.silu(cond_slab).astype(BF16)
        partial_mod = dot32("sd,lmdc->lmsc", silu_slab, w_mod)
        partial_mod = partial_mod.reshape(
            layer_count * 2, micro_count, n_tensor, own_rows * column_count
        )
        partial_mod = partial_mod.transpose(2, 0, 1, 3).reshape(n_tensor, -1, column_count)
        partial_mod = lax.all_to_all(partial_mod, "tensor", 0, 0, tiled=True)
        attn_own, partial_mod = tied(attn_shards[0], partial_mod)
        attn_others = with_blocks(attn_own[0])[1:]
        partial_mod = axis_sum(partial_mod, "dp")
        mod_own = partial_mod.transpose(1, 0, 2)
        mod_own = mod_own.reshape(layer_count, 2, seqs, 6, model_width)
    rest, first_attn, mod_own = tied(attn_others, first_attn, mod_own)
    attn_w = (first_attn, gather_pages(jnp.concatenate(rest, axis=0)))
    mods = [[mod_own[layer_at, u] for u in range(2)] for layer_at in range(layer_count)]

    def rows_in(values):
        return values.reshape(seqs, values.shape[2], model_width).astype(F32)

    def rows_out(values):
        return values.reshape(micro_count, own_rows, values.shape[1], model_width)

    streams = [rows_in(image_in), rows_in(text_in)]
    saved, weights = [], []
    for layer_at in range(layer_count):
        streams, kept, gathered, attn_w = forward_layer(
            streams,
            mods[layer_at],
            attn_w,
            all_mlp_shards[layer_at],
            attn_shards[layer_at + 1] if layer_at + 1 < layer_count else [],
        )
        weights.append(gathered)
        saved.append(kept)
    grads_now = [rows_in(cot_image), rows_in(cot_text)]
    shards = [None] * layer_count
    d_mods = [None] * layer_count
    pending = None
    for layer_at in reversed(range(layer_count)):
        grads_now, d_mods[layer_at], slabs, done = backward_layer(
            grads_now, mods[layer_at], weights[layer_at], saved[layer_at], pending, layer_at == 0
        )
        if pending:
            shards[layer_at + 1] = done
        pending = slabs
    with jax.named_scope("modulation_grad"):
        d_mods = jnp.concatenate(d_mods).reshape(layer_count * 2 * seqs, n_tensor, column_count)
        d_mods = lax.all_to_all(d_mods.transpose(1, 0, 2), "tensor", 0, 0, tiled=True)
        attn_slab, d_mods = tied(pending[1], d_mods)
        shards[0] = (
            mlp_shard(pending[0], n_tensor // 2),
            attention_shard(attn_slab, n_tensor // 2),
        )
        d_mods = axis_sum(d_mods, "dp")
        d_mods = d_mods.reshape(n_tensor, layer_count, 2, micro_count, own_rows, column_count)
        d_columns = d_mods.transpose(1, 2, 3, 0, 4, 5)
        d_columns = d_columns.reshape(layer_count, 2, -1, column_count)
        grad_w_mod = jnp.einsum(
            "sd,lmsc->lmdc",
            silu_slab.astype(F32),
            d_columns,
            precision=HIGHEST,
            preferred_element_type=F32,
        )
        d_silu = jnp.einsum(
            "lmsc,lmdc->sd",
            d_columns,
            w_mod.astype(F32),
            precision=HIGHEST,
            preferred_element_type=F32,
        )
    with jax.named_scope("conditioning_grad"):
        d_cond = jax.vjp(jax.nn.silu, cond_slab)[1](d_silu)[0]
        grad_cond = axis_sum(
            jnp.dot(onehot.T, d_cond, precision=HIGHEST, preferred_element_type=F32), "tensor"
        )
    with jax.named_scope("weight_grads"):
        stacked = [
            jnp.stack([layer[part][at] for layer in shards])
            for part, at in ((1, 0), (1, 1), (0, 0), (0, 1))
        ]
    return (
        rows_out(streams[0].astype(BF16)),
        rows_out(streams[1].astype(BF16)),
        rows_out(grads_now[0]),
        rows_out(grads_now[1]),
        grad_cond,
        grad_w_mod,
        *stacked,
    )


def solution(mesh):
    rows = P(None, "tensor", "dp", None)
    up_like = P(None, None, "dp", "tensor")
    down_like = P(None, None, "tensor", "dp")
    qkv_like = P(None, None, None, "dp", "tensor")
    return jax.shard_map(
        per_device,
        mesh=mesh,
        in_specs=(
            rows,
            rows,
            P(),
            P(),
            up_like,
            qkv_like,
            down_like,
            up_like,
            down_like,
            rows,
            rows,
        ),
        out_specs=(
            rows,
            rows,
            rows,
            rows,
            P(None, "dp"),
            up_like,
            qkv_like,
            down_like,
            up_like,
            down_like,
        ),
        check_vma=False,
    )
```

```python
import functools

import jax
import jax.numpy as jnp
from jax import lax
from jax.experimental import pallas as pl
from jax.experimental.layout import Layout, with_layout_constraint
from jax.experimental.pallas import tpu as pltpu
from jax.sharding import PartitionSpec as P

HDIM = 64
LANES = 128
EPS = 1e-06
HIGHEST = lax.Precision.HIGHEST
BF16 = jnp.bfloat16
F32 = jnp.float32


def dot32(pattern, left, right):
    return jnp.einsum(pattern, left, right, preferred_element_type=F32)


def tensor_swap(values, distance):
    count = lax.axis_size("tensor")
    return lax.ppermute(values, "tensor", [(i, i ^ distance) for i in range(count)])


def pair_swap(values):
    return tensor_swap(values, 1)


def hi_swap(values, block):
    return tensor_swap(values, 2 * block)


def axis_sum(values, axis):
    count = lax.axis_size(axis)
    step = 1
    while step < count:
        values = values + lax.ppermute(values, axis, [(i, i ^ step) for i in range(count)])
        step *= 2
    return values


def rows_of_others(image, text):
    image_rows = image.shape[1]
    image, text = tied(image, text)
    received = pair_swap(jnp.concatenate([image, text], axis=1))
    far = [tensor_swap(text, at) for at in range(2, lax.axis_size("tensor"))]
    return (image, received[:, :image_rows]), jnp.stack([text, received[:, image_rows:], *far])


def sum_over_others(image_own, image_other, text_terms, *meanwhile):
    image_rows = image_own.shape[1]
    sent = jnp.concatenate([image_other.astype(BF16), text_terms[1].astype(BF16)], axis=1)
    received = pair_swap(sent)
    far = [
        tensor_swap(text_terms[at].astype(BF16), at) for at in range(2, text_terms.shape[0])
    ]
    received, far, *meanwhile = tied(received, far, *meanwhile)
    image = image_own + received[:, :image_rows].astype(F32)
    text = text_terms[0] + received[:, image_rows:].astype(F32)
    for part in far:
        text = text + part.astype(F32)
    return [image, text], *meanwhile


def to_sequences(parts, blocks):
    received = [parts[:2]] + [
        hi_swap(parts[2 * block : 2 * block + 2], block) for block in range(1, blocks)
    ]
    return [flat_pairs(part) for part in received]


def to_blocks(by_block, seqs):
    split = [part.reshape(2, seqs, *part.shape[1:]) for part in by_block]
    parts = [split[0]] + [hi_swap(split[block], block) for block in range(1, len(split))]
    return jnp.concatenate(parts, axis=0)


def flat_pairs(values):
    return values.reshape(-1, *values.shape[2:])


def head_mask(rows, which):
    lane = lax.broadcasted_iota(jnp.int32, (rows, LANES), 1)
    return (lane < HDIM) if which == 0 else (lane >= HDIM)


def nt_dot(left, right):
    return lax.dot_general(left, right, (((1,), (1,)), ((), ())), preferred_element_type=F32)


def attn_fwd_kernel(q_ref, k_ref, v_ref, o_ref, lse_ref):
    rows = q_ref.shape[0]
    queries = q_ref[...] * jnp.asarray(HDIM ** (-0.5), BF16)
    keys = k_ref[...]
    values_t = v_ref[...].astype(F32).T.astype(BF16)
    parts = []
    for which in range(2):
        masked = jnp.where(head_mask(rows, which), queries, jnp.zeros_like(queries))
        scores = nt_dot(keys, masked)
        peak = jnp.max(scores, axis=0, keepdims=True)
        raised = jnp.exp(scores - peak)
        total = jnp.sum(raised, axis=0, keepdims=True)
        out_t = jnp.dot(
            values_t[which * HDIM : (which + 1) * HDIM],
            raised.astype(BF16),
            preferred_element_type=F32,
        )
        parts.append(out_t * (1.0 / total))
        lse_ref[0, 0, which : which + 1, :] = peak + jnp.log(total)
    o_ref[...] = jnp.concatenate(parts, axis=0).T.astype(BF16)


def attn_bwd_kernel(q_ref, k_ref, v_ref, do_ref, lse_ref, dq_ref, dk_ref, dv_ref, dk_acc, dv_acc):
    tile = pl.program_id(1)
    rows = q_ref.shape[0]
    scale = HDIM ** (-0.5)

    @pl.when(tile == 0)
    def _():
        dk_acc[...] = jnp.zeros_like(dk_acc)
        dv_acc[...] = jnp.zeros_like(dv_acc)

    queries = q_ref[...] * jnp.asarray(scale, BF16)
    d_out = do_ref[...]
    keys = k_ref[...]
    values = v_ref[...]
    keys_t = keys.astype(F32).T.astype(BF16)
    parts = []
    for which in range(2):
        mask = head_mask(rows, which)
        q_masked = jnp.where(mask, queries, jnp.zeros_like(queries))
        do_masked = jnp.where(mask, d_out, jnp.zeros_like(d_out))
        scores = nt_dot(keys, q_masked)
        probs = jnp.exp(scores - lse_ref[0, 0, which : which + 1, :])
        d_probs = nt_dot(values, do_masked)
        centre = jnp.sum(probs * d_probs, axis=0, keepdims=True)
        d_scores = (probs * (d_probs - centre)).astype(BF16)
        dv_acc[...] += jnp.dot(probs.astype(BF16), do_masked, preferred_element_type=F32)
        dk_acc[...] += jnp.dot(d_scores, q_masked, preferred_element_type=F32)
        parts.append(
            jnp.dot(
                keys_t[which * HDIM : (which + 1) * HDIM], d_scores, preferred_element_type=F32
            )
        )
    dq_ref[...] = (jnp.concatenate(parts, axis=0).T * scale).astype(BF16)

    @pl.when(tile == pl.num_programs(1) - 1)
    def _():
        dk_ref[...] = dk_acc[...].astype(BF16)
        dv_ref[...] = dv_acc[...].astype(BF16)


def query_rows(length):
    return length // 2 if length % 32 == 0 else length


def padded_columns(columns):
    return -(-columns // LANES) * LANES


def pad_heads(packed, pieces):
    columns = packed.shape[1] // pieces
    wide = padded_columns(columns)
    if wide == columns:
        return packed
    split = packed.reshape(packed.shape[0], pieces, columns)
    return jnp.pad(split, ((0, 0), (0, 0), (0, wide - columns))).reshape(
        packed.shape[0], pieces * wide
    )


def attention_forward(packed):
    length = packed.shape[0]
    columns = packed.shape[1] // 3
    wide = padded_columns(columns)
    pairs = wide // LANES
    rows = query_rows(length)
    tiles = length // rows
    packed = pad_heads(packed, 3)
    mixed, lse = pl.pallas_call(
        attn_fwd_kernel,
        grid=(pairs, tiles),
        in_specs=[
            pl.BlockSpec((rows, LANES), lambda p, t: (t, p)),
            pl.BlockSpec((length, LANES), lambda p, t: (0, pairs + p)),
            pl.BlockSpec((length, LANES), lambda p, t: (0, 2 * pairs + p)),
        ],
        out_specs=[
            pl.BlockSpec((rows, LANES), lambda p, t: (t, p)),
            pl.BlockSpec((1, 1, 8, rows), lambda p, t: (p, t, 0, 0)),
        ],
        out_shape=[
            jax.ShapeDtypeStruct((length, wide), BF16),
            jax.ShapeDtypeStruct((pairs, tiles, 8, rows), F32),
        ],
        compiler_params=pltpu.CompilerParams(vmem_limit_bytes=40 * 1024 * 1024),
        cost_estimate=pl.CostEstimate(
            flops=8 * length * length * wide,
            bytes_accessed=8 * length * wide,
            transcendentals=length * length * wide // HDIM,
        ),
    )(packed, packed, packed)
    return mixed[:, :columns], lse


def attention_backward(packed, d_mixed, lse):
    length = packed.shape[0]
    columns = packed.shape[1] // 3
    wide = padded_columns(columns)
    pairs = wide // LANES
    rows = query_rows(length)
    tiles = length // rows
    packed = pad_heads(packed, 3)
    d_mixed = pad_heads(d_mixed, 1)
    grads = pl.pallas_call(
        attn_bwd_kernel,
        grid=(pairs, tiles),
        in_specs=[
            pl.BlockSpec((rows, LANES), lambda p, t: (t, p)),
            pl.BlockSpec((length, LANES), lambda p, t: (0, pairs + p)),
            pl.BlockSpec((length, LANES), lambda p, t: (0, 2 * pairs + p)),
            pl.BlockSpec((rows, LANES), lambda p, t: (t, p)),
            pl.BlockSpec((1, 1, 8, rows), lambda p, t: (p, t, 0, 0)),
        ],
        out_specs=[
            pl.BlockSpec((rows, LANES), lambda p, t: (t, p)),
            pl.BlockSpec((length, LANES), lambda p, t: (0, p)),
            pl.BlockSpec((length, LANES), lambda p, t: (0, p)),
        ],
        out_shape=[jax.ShapeDtypeStruct((length, wide), BF16)] * 3,
        scratch_shapes=[pltpu.VMEM((length, LANES), F32)] * 2,
        compiler_params=pltpu.CompilerParams(vmem_limit_bytes=48 * 1024 * 1024),
        cost_estimate=pl.CostEstimate(
            flops=20 * length * length * wide,
            bytes_accessed=14 * length * wide,
            transcendentals=length * length * wide // HDIM,
        ),
    )(packed, packed, packed, d_mixed, lse)
    return jnp.concatenate([part[:, :columns] for part in grads], axis=1)


def normalized(values_in):
    centre = jnp.mean(values_in, axis=-1, keepdims=True)
    offsets = values_in - centre
    spread = jnp.mean(offsets * offsets, axis=-1, keepdims=True)
    factor = lax.rsqrt(spread + EPS)
    return offsets * factor, factor


def modulate(values_in, mod_rows, first):
    normal, _ = normalized(values_in)
    shift = mod_rows[:, first][:, None]
    scale = mod_rows[:, first + 1][:, None]
    return (normal * (1.0 + scale) + shift).astype(BF16)


def modulate_backward(values_in, d_out, mod_rows, first):
    normal, factor = normalized(values_in)
    scale = mod_rows[:, first + 1][:, None]
    d_shift = jnp.sum(d_out, axis=1)
    d_scale = jnp.sum(d_out * normal, axis=1)
    d_normal = d_out * (1.0 + scale)
    mean_plain = jnp.mean(d_normal, axis=-1, keepdims=True)
    mean_along = jnp.mean(d_normal * normal, axis=-1, keepdims=True)
    return (d_normal - mean_plain - normal * mean_along) * factor, d_shift, d_scale


def gelu_tanh(values_in):
    return jax.nn.gelu(values_in, approximate=True)


def tied(values, *others):
    return lax.optimization_barrier((values, *others))


def both(own, other):
    return jnp.concatenate([own, other], axis=0)


def rows_dot(rows, page):
    return dot32("...d,df->...f", rows, page)


def back_dot(rows, page):
    return dot32("...f,df->...d", rows, page)


def back_sum(rows_list, pages):
    return sum(back_dot(rows, page) for rows, page in zip(rows_list, pages))


def flat(values):
    return values.reshape(-1, values.shape[-1])


def row_major(values):
    return with_layout_constraint(values, Layout(major_to_minor=tuple(range(values.ndim))))


def page_grad(left, right):
    grad = lax.dot_general(
        flat(left), flat(right), (((0,), (0,)), ((), ())), preferred_element_type=F32
    )
    return row_major(grad.astype(BF16))


def token_halves(values, seqs):
    return values[:seqs], values[seqs:]


def to_attention(image_parts, text_parts):
    packed = [
        jnp.concatenate([image, text], axis=1) for image, text in zip(image_parts, text_parts)
    ]
    packed = jnp.stack(packed, axis=1)
    return packed.reshape(-1, *packed.shape[2:])


def from_attention(values, blocks, image_rows):
    values = values.reshape(-1, blocks, *values.shape[1:])
    image = [values[:, block, :image_rows] for block in range(blocks)]
    text = [values[:, block, image_rows:] for block in range(blocks)]
    return image, text


def mlp_result(image_act, text_act, down_w, middle, mods):
    other = back_sum(image_act[1], down_w[0]).astype(BF16)
    text_terms = back_dot(text_act, down_w[1][0])
    own = back_sum(image_act[0], down_w[0])
    (mlp,) = sum_over_others(own, other, text_terms)
    return mlp, [middle[u] + mods[u][:, 5][:, None] * mlp[u] for u in range(2)]


def forward_layer(streams, mods, attn_w, mlp_shards, next_shards, early):
    seqs, image_rows = streams[0].shape[:2]
    with jax.named_scope("attention"):
        normed = [modulate(streams[u], mods[u], 0) for u in range(2)]
        image_one, text_one = rows_of_others(*normed)
        image_shards = jnp.concatenate([mlp_shards[0], *next_shards[:1]], axis=0)
        mlp_shards = jnp.concatenate(mlp_shards, axis=0)
        text_one, mlp_shards, image_shards = tied(text_one, mlp_shards, image_shards)
        mlp_w = [gather_pages(mlp_shards)]
        others = with_blocks(image_shards)[1:]
        qkv_w, out_w = attention_pages(attn_w)
        blocks = len(qkv_w[0])
        text_heads = rows_dot(text_one, qkv_w[1][0]).astype(BF16)
        text_heads = to_sequences(text_heads, blocks)
        image_heads = [
            both(*[rows_dot(part, page).astype(BF16) for part in image_one]) for page in qkv_w[0]
        ]
        packed = to_attention(image_heads, text_heads)
        tokens, columns = packed.shape[1:]
        if early:
            early, packed = tied(early, packed)
            early = rows_of_others(*early)
        packed = lax.all_to_all(packed, "dp", 0, 0, tiled=True)
        packed = packed.reshape(-1, columns)
        mixed, lse = attention_forward(packed)
        mixed = mixed.reshape(-1, tokens, columns // 3)
        mixed = lax.all_to_all(mixed, "dp", 0, 0, tiled=True)
        mixed, others, early = tied(mixed, others, early)
        others, mlp_w[0] = tied(others, mlp_w[0])
        mlp_w.append(gather_pages(jnp.concatenate([part[:2] for part in others], axis=0)))
        next_others = [part[2:] for part in others]
        image_mixed, text_mixed = from_attention(mixed, blocks, image_rows)
        text_mixed = to_blocks(text_mixed, seqs)
        other = back_sum([part[seqs:] for part in image_mixed], out_w[0])
        text_terms = back_dot(text_mixed, out_w[1][0])
        own = back_sum([part[:seqs] for part in image_mixed], out_w[0])
        (attn,) = sum_over_others(own, other, text_terms)
    with jax.named_scope("mlp"):
        middle = [streams[u] + mods[u][:, 2][:, None] * attn[u] for u in range(2)]
        normed_two = [modulate(middle[u], mods[u], 3) for u in range(2)]
        image_two, text_two = rows_of_others(*normed_two)
        up_w, down_w = mlp_pages(mlp_w)
        image_up = [[rows_dot(part, page) for page in up_w[0]] for part in image_two]
        next_attn = None
        if next_shards:
            image_up[0][0], mlp_w[1], next_shards, next_others = tied(
                image_up[0][0], mlp_w[1], next_shards, next_others
            )
            next_attn = (gather_pages(jnp.concatenate([*next_shards, *next_others], axis=0)),)
        image_act = [[gelu_tanh(up).astype(BF16) for up in part] for part in image_up]
        text_up = rows_dot(text_two, up_w[1][0])
        text_act = gelu_tanh(text_up).astype(BF16)
        mlp = result = None
        if not early:
            mlp, result = mlp_result(image_act, text_act, down_w, middle, mods)
    saved = dict(
        streams=streams,
        image_one=both(*image_one),
        text_one=text_one,
        packed=packed,
        lse=lse,
        image_mixed=image_mixed,
        text_mixed=text_mixed,
        attn=attn,
        middle=middle,
        image_two=both(*image_two),
        text_two=text_two,
        image_up=image_up,
        image_act=image_act,
        text_up=text_up,
        text_act=text_act,
        mlp=mlp,
    )
    return result, saved, (attn_w, mlp_w), next_attn, early


def gelu_pull(up_values, d_active):
    return jax.vjp(gelu_tanh, up_values)[1](d_active)[0].astype(BF16)


def scatter_pages(wide):
    return lax.psum_scatter(wide, "dp", scatter_dimension=0, tiled=True)


def send_blocks(slab, blocks):
    width = slab.shape[1] // (blocks + 1)
    parts = [slab[:, (block + 1) * width : (block + 2) * width] for block in range(1, blocks)]
    return [slab[:, : 2 * width]] + [hi_swap(part, at + 1) for at, part in enumerate(parts)]


def shard_rows(parts):
    width = parts[0].shape[1] // 2
    image = parts[0][:, :width].astype(F32)
    for part in parts[1:]:
        image = image + part.astype(F32)
    return image, parts[0][:, width:].astype(F32)


def page_list(image_first, image_second, text_first, text_second):
    pages = [image_first[0], image_second[0], text_first, text_second]
    for pair in zip(image_first[1:], image_second[1:]):
        pages += pair
    return pages


def mlp_shard(parts):
    rows = shard_rows(parts)
    half = rows[0].shape[1] // 2
    return (
        jnp.stack([part[:, half:] for part in rows]),
        jnp.stack([part[:, :half].T for part in rows]),
    )


def attention_shard(parts):
    rows = shard_rows(parts)
    columns = rows[0].shape[1] // 4
    return (
        jnp.stack(
            [
                jnp.stack([part[:, at * columns : (at + 1) * columns] for at in range(3)])
                for part in rows
            ]
        ),
        jnp.stack([part[:, 3 * columns :].T for part in rows]),
    )


def gated_rows(rows, mods, gate):
    return [(mods[u][:, gate][:, None] * rows[u]).astype(BF16) for u in range(2)]


def backward_layer(grads_out, mods, weights, saved, pending, final, dmlp):
    seqs, image_rows = grads_out[0].shape[:2]
    qkv_w, out_w = attention_pages(weights[0])
    up_w, down_w = mlp_pages(weights[1])
    blocks = len(qkv_w[0])
    middle, attn, mlp = saved["middle"], saved["attn"], saved["mlp"]
    with jax.named_scope("mlp_grad"):
        image_dmlp, text_dmlp = dmlp or rows_of_others(*gated_rows(grads_out, mods, 5))
        image_dup = [
            [
                gelu_pull(saved["image_up"][at][block], rows_dot(image_dmlp[at], down_w[0][block]))
                for block in range(blocks)
            ]
            for at in range(2)
        ]
        other = back_sum(image_dup[1], up_w[0])
        text_dup = gelu_pull(saved["text_up"], rows_dot(text_dmlp, down_w[1][0]))
        text_terms = back_dot(text_dup, up_w[1][0])
        own = back_sum(image_dup[0], up_w[0])
        dmlp_rows = both(*image_dmlp)
        grads = page_list(
            [page_grad(dmlp_rows, both(*parts)) for parts in zip(*saved["image_act"])],
            [page_grad(saved["image_two"], both(*parts)) for parts in zip(*image_dup)],
            page_grad(text_dmlp, saved["text_act"]),
            page_grad(saved["text_two"], text_dup),
        )
        wide = jnp.concatenate(grads, axis=1)
        d_two, wide = sum_over_others(own, other, text_terms, wide)
        mlp_slab = scatter_pages(wide)
        d_middle, d_shift_two, d_scale_two = [], [], []
        for u in range(2):
            d_values, d_shift, d_scale = modulate_backward(middle[u], d_two[u], mods[u], 3)
            d_middle.append(grads_out[u] + d_values)
            d_shift_two.append(d_shift)
            d_scale_two.append(d_scale)
    with jax.named_scope("attention_grad"):
        image_dattn, text_dattn = rows_of_others(*gated_rows(d_middle, mods, 2))
        d_gate_one = [jnp.sum(d_middle[u] * attn[u], axis=1) for u in range(2)]
        text_dmixed = to_sequences(rows_dot(text_dattn, out_w[1][0]).astype(BF16), blocks)
        image_dmixed = [
            both(*[rows_dot(part, page).astype(BF16) for part in image_dattn]) for page in out_w[0]
        ]
        d_mixed = to_attention(image_dmixed, text_dmixed)
        tokens, columns = d_mixed.shape[1:]
        result = None
        if mlp is None:
            late, d_mixed = tied((saved["image_act"], saved["text_act"]), d_mixed)
            mlp, result = mlp_result(*late, down_w, middle, mods)
        d_mixed = lax.all_to_all(d_mixed, "dp", 0, 0, tiled=True)
        done = []
        if pending:
            mlp_before, d_mixed = tied(pending[0], d_mixed)
            done.append(mlp_shard(send_blocks(mlp_before, blocks)))
        d_mixed = d_mixed.reshape(-1, columns)
        d_packed = attention_backward(saved["packed"], d_mixed, saved["lse"])
        if pending:
            attn_before, d_packed = tied(pending[1], d_packed)
            attn_before = send_blocks(attn_before, blocks)
        d_packed = d_packed.reshape(-1, tokens, 3 * columns)
        d_packed = lax.all_to_all(d_packed, "dp", 0, 0, tiled=True)
        if pending:
            done[0], attn_before, d_packed = tied(done[0], attn_before, d_packed)
            done.append(attention_shard(attn_before))
        if result:
            mlp, result, d_packed = tied(mlp, result, d_packed)
        d_gate_two = [jnp.sum(grads_out[u] * mlp[u], axis=1) for u in range(2)]
        image_dproj, text_dproj = from_attention(d_packed, blocks, image_rows)
        text_dproj = to_blocks(text_dproj, seqs)
        grad_rows = image_dproj
        if not final:
            other = back_sum([part[seqs:] for part in image_dproj], qkv_w[0]).astype(BF16)
            grad_rows, other = tied(image_dproj, other)
        dattn_rows = both(*image_dattn)
        grads = page_list(
            [page_grad(saved["image_one"], part) for part in grad_rows],
            [page_grad(dattn_rows, part) for part in saved["image_mixed"]],
            page_grad(saved["text_one"], text_dproj),
            page_grad(text_dattn, saved["text_mixed"]),
        )
        wide = jnp.concatenate(grads, axis=1)
        if final:
            wide, image_dproj = tied(wide, image_dproj)
            other = back_sum([part[seqs:] for part in image_dproj], qkv_w[0]).astype(BF16)
        text_terms = back_dot(text_dproj, qkv_w[1][0])
        own = back_sum([part[:seqs] for part in image_dproj], qkv_w[0])
        (d_one,) = sum_over_others(own, other, text_terms)
        wide, mlp_slab = tied(wide, mlp_slab)
        attn_slab = scatter_pages(wide)
        d_inputs, d_mods = [], []
        for u in range(2):
            d_values, d_shift, d_scale = modulate_backward(
                saved["streams"][u], d_one[u], mods[u], 0
            )
            d_inputs.append(d_middle[u] + d_values)
            d_mods.append(
                jnp.concatenate(
                    [d_shift, d_scale, d_gate_one[u], d_shift_two[u], d_scale_two[u], d_gate_two[u]],
                    axis=1,
                )
            )
    return d_inputs, jnp.concatenate(d_mods), (mlp_slab, attn_slab), done, result


def with_blocks(pages):
    hi_count = lax.axis_size("tensor") // 2
    return [pages] + [hi_swap(pages, block) for block in range(1, hi_count)]


def gather_pages(pages):
    return lax.all_gather(pages, "dp", axis=1, tiled=True)


def attn_page(w_qkv, w_out, layer_at, u):
    qkv = w_qkv[layer_at, u].transpose(1, 0, 2)
    qkv = qkv.reshape(qkv.shape[0], -1)
    return jnp.concatenate([qkv, w_out[layer_at, u].T], axis=1)


def attention_shards(w_qkv, w_out, layer_at):
    return [attn_page(w_qkv, w_out, layer_at, u)[None] for u in range(2)]


def mlp_shards(w_up, w_down, layer_at):
    return [jnp.stack([w_up[layer_at, u], w_down[layer_at, u].T]) for u in range(2)]


def attention_pages(gathered):
    pages = [pages[at] for pages in gathered for at in range(pages.shape[0])]
    qkv_columns = pages[0].shape[1] * 3 // 4
    by_stream = [[pages[0], *pages[2:]], [pages[1]]]
    qkv_w = [[page[:, :qkv_columns] for page in group] for group in by_stream]
    out_w = [[page[:, qkv_columns:] for page in group] for group in by_stream]
    return qkv_w, out_w


def mlp_pages(gathered):
    pages = [pages[at] for pages in gathered for at in range(pages.shape[0])]
    by_stream = [[*pages[:2], *pages[4:]], pages[2:4]]
    return [group[0::2] for group in by_stream], [group[1::2] for group in by_stream]


def per_device(
    image_in,
    text_in,
    cond_table,
    cond_index,
    w_mod,
    w_qkv,
    w_out,
    w_up,
    w_down,
    cot_image,
    cot_text,
):
    n_tensor = lax.axis_size("tensor")
    dp_at = lax.axis_index("dp")
    micro_count, own_rows = image_in.shape[:2]
    seqs = micro_count * own_rows
    model_width = image_in.shape[3]
    layer_count = w_qkv.shape[0]
    slab_rows = w_mod.shape[2]
    column_count = w_mod.shape[3]
    index_flat = cond_index.reshape(-1)
    attn_shards = [attention_shards(w_qkv, w_out, at) for at in range(layer_count)]
    all_mlp_shards = [mlp_shards(w_up, w_down, at) for at in range(layer_count)]
    first_attn = gather_pages(jnp.concatenate(attn_shards[0], axis=0))
    with jax.named_scope("modulation"):
        onehot = (
            index_flat[:, None] == jnp.arange(cond_table.shape[0], dtype=jnp.int32)[None, :]
        ).astype(F32)
        cond_slab = lax.dynamic_slice_in_dim(cond_table, dp_at * slab_rows, slab_rows, 1)
        cond_slab = jnp.dot(onehot, cond_slab, precision=HIGHEST, preferred_element_type=F32)
        silu_slab = jax.nn.silu(cond_slab).astype(BF16)
        partial_mod = dot32("sd,lmdc->lmsc", silu_slab, w_mod)
        partial_mod = partial_mod.reshape(
            layer_count * 2, micro_count, n_tensor, own_rows * column_count
        )
        partial_mod = partial_mod.transpose(2, 0, 1, 3).reshape(n_tensor, -1, column_count)
        partial_mod = lax.all_to_all(partial_mod, "tensor", 0, 0, tiled=True)
        attn_own, partial_mod = tied(attn_shards[0], partial_mod)
        attn_others = with_blocks(attn_own[0])[1:]
        partial_mod = axis_sum(partial_mod, "dp")
        mod_own = partial_mod.transpose(1, 0, 2)
        mod_own = mod_own.reshape(layer_count, 2, seqs, 6, model_width)
    rest, first_attn, mod_own = tied(attn_others, first_attn, mod_own)
    attn_w = (first_attn, gather_pages(jnp.concatenate(rest, axis=0)))
    mods = [[mod_own[layer_at, u] for u in range(2)] for layer_at in range(layer_count)]

    def rows_in(values):
        return values.reshape(seqs, values.shape[2], model_width).astype(F32)

    def rows_out(values):
        return values.reshape(micro_count, own_rows, values.shape[1], model_width)

    streams = [rows_in(image_in), rows_in(text_in)]
    grads_now = [rows_in(cot_image), rows_in(cot_text)]
    saved, weights = [], []
    for layer_at in range(layer_count):
        last = layer_at + 1 == layer_count
        streams, kept, gathered, attn_w, dmlp = forward_layer(
            streams,
            mods[layer_at],
            attn_w,
            all_mlp_shards[layer_at],
            [] if last else attn_shards[layer_at + 1],
            gated_rows(grads_now, mods[layer_at], 5) if last else (),
        )
        weights.append(gathered)
        saved.append(kept)
    shards = [None] * layer_count
    d_mods = [None] * layer_count
    pending = None
    for layer_at in reversed(range(layer_count)):
        grads_now, d_mods[layer_at], slabs, done, result = backward_layer(
            grads_now,
            mods[layer_at],
            weights[layer_at],
            saved[layer_at],
            pending,
            layer_at == 0,
            dmlp,
        )
        dmlp = None
        streams = result or streams
        if pending:
            shards[layer_at + 1] = done
        pending = slabs
    with jax.named_scope("modulation_grad"):
        d_mods = jnp.concatenate(d_mods).reshape(layer_count * 2 * seqs, n_tensor, column_count)
        d_mods = lax.all_to_all(d_mods.transpose(1, 0, 2), "tensor", 0, 0, tiled=True)
        blocks = n_tensor // 2
        mlp_parts = send_blocks(pending[0], blocks)
        mlp_parts, attn_slab = tied(mlp_parts, pending[1])
        attn_parts = send_blocks(attn_slab, blocks)
        d_mods = axis_sum(d_mods, "dp")
        d_mods = d_mods.reshape(n_tensor, layer_count, 2, micro_count, own_rows, column_count)
        d_columns = d_mods.transpose(1, 2, 3, 0, 4, 5)
        d_columns = d_columns.reshape(layer_count, 2, -1, column_count)
        grad_w_mod = jnp.einsum(
            "sd,lmsc->lmdc",
            silu_slab.astype(F32),
            d_columns,
            precision=HIGHEST,
            preferred_element_type=F32,
        )
        d_silu = jnp.einsum(
            "lmsc,lmdc->sd",
            d_columns,
            w_mod.astype(F32),
            precision=HIGHEST,
            preferred_element_type=F32,
        )
    with jax.named_scope("conditioning_grad"):
        d_cond = jax.vjp(jax.nn.silu, cond_slab)[1](d_silu)[0]
        grad_cond = axis_sum(
            jnp.dot(onehot.T, d_cond, precision=HIGHEST, preferred_element_type=F32), "tensor"
        )
    with jax.named_scope("weight_grads"):
        mlp_done = [mlp_shard(mlp_parts)] + [layer[0] for layer in shards[1:]]
        grad_up, grad_down = [jnp.stack(parts) for parts in zip(*mlp_done)]
        attn_parts, grad_up, grad_down, grad_w_mod, grad_cond = tied(
            attn_parts, grad_up, grad_down, grad_w_mod, grad_cond
        )
        attn_done = [attention_shard(attn_parts)] + [layer[1] for layer in shards[1:]]
        grad_qkv, grad_out = [jnp.stack(parts) for parts in zip(*attn_done)]
    return (
        rows_out(streams[0].astype(BF16)),
        rows_out(streams[1].astype(BF16)),
        rows_out(grads_now[0]),
        rows_out(grads_now[1]),
        grad_cond,
        grad_w_mod,
        grad_qkv,
        grad_out,
        grad_up,
        grad_down,
    )


def solution(mesh):
    rows = P(None, "tensor", "dp", None)
    up_like = P(None, None, "dp", "tensor")
    down_like = P(None, None, "tensor", "dp")
    qkv_like = P(None, None, None, "dp", "tensor")
    return jax.shard_map(
        per_device,
        mesh=mesh,
        in_specs=(
            rows,
            rows,
            P(),
            P(),
            up_like,
            qkv_like,
            down_like,
            up_like,
            down_like,
            rows,
            rows,
        ),
        out_specs=(
            rows,
            rows,
            rows,
            rows,
            P(None, "dp"),
            up_like,
            qkv_like,
            down_like,
            up_like,
            down_like,
        ),
        check_vma=False,
    )
```

```python
import functools

import jax
import jax.numpy as jnp
from jax import lax
from jax.experimental import pallas as pl
from jax.experimental.layout import Layout, with_layout_constraint
from jax.experimental.pallas import tpu as pltpu
from jax.sharding import PartitionSpec as P

HDIM = 64
LANES = 128
EPS = 1e-06
HIGHEST = lax.Precision.HIGHEST
BF16 = jnp.bfloat16
F32 = jnp.float32


def dot32(pattern, left, right):
    return jnp.einsum(pattern, left, right, preferred_element_type=F32)


def tensor_swap(values, distance):
    count = lax.axis_size("tensor")
    return lax.ppermute(values, "tensor", [(i, i ^ distance) for i in range(count)])


def pair_swap(values):
    return tensor_swap(values, 1)


def hi_swap(values, block):
    return tensor_swap(values, 2 * block)


def axis_sum(values, axis):
    count = lax.axis_size(axis)
    step = 1
    while step < count:
        values = values + lax.ppermute(values, axis, [(i, i ^ step) for i in range(count)])
        step *= 2
    return values


def rows_of_others(image, text):
    image_rows = image.shape[1]
    image, text = tied(image, text)
    received = pair_swap(jnp.concatenate([image, text], axis=1))
    far = [tensor_swap(text, at) for at in range(2, lax.axis_size("tensor"))]
    return (image, received[:, :image_rows]), jnp.stack([text, received[:, image_rows:], *far])


def sum_over_others(image_own, image_other, text_terms, *meanwhile):
    image_rows = image_own.shape[1]
    sent = jnp.concatenate([image_other.astype(BF16), text_terms[1].astype(BF16)], axis=1)
    received = pair_swap(sent)
    far = [
        tensor_swap(text_terms[at].astype(BF16), at) for at in range(2, text_terms.shape[0])
    ]
    received, far, *meanwhile = tied(received, far, *meanwhile)
    image = image_own + received[:, :image_rows].astype(F32)
    text = text_terms[0] + received[:, image_rows:].astype(F32)
    for part in far:
        text = text + part.astype(F32)
    return [image, text], *meanwhile


def to_sequences(parts, blocks):
    received = [parts[:2]] + [
        hi_swap(parts[2 * block : 2 * block + 2], block) for block in range(1, blocks)
    ]
    return [flat_pairs(part) for part in received]


def to_blocks(by_block, seqs):
    split = [part.reshape(2, seqs, *part.shape[1:]) for part in by_block]
    parts = [split[0]] + [hi_swap(split[block], block) for block in range(1, len(split))]
    return jnp.concatenate(parts, axis=0)


def flat_pairs(values):
    return values.reshape(-1, *values.shape[2:])


def head_mask(rows, which):
    lane = lax.broadcasted_iota(jnp.int32, (rows, LANES), 1)
    return (lane < HDIM) if which == 0 else (lane >= HDIM)


def nt_dot(left, right):
    return lax.dot_general(left, right, (((1,), (1,)), ((), ())), preferred_element_type=F32)


def attn_fwd_kernel(q_ref, k_ref, v_ref, o_ref, lse_ref):
    rows = q_ref.shape[0]
    queries = q_ref[...] * jnp.asarray(HDIM ** (-0.5), BF16)
    keys = k_ref[...]
    values_t = v_ref[...].astype(F32).T.astype(BF16)
    parts = []
    for which in range(2):
        masked = jnp.where(head_mask(rows, which), queries, jnp.zeros_like(queries))
        scores = nt_dot(keys, masked)
        peak = jnp.max(scores, axis=0, keepdims=True)
        raised = jnp.exp(scores - peak)
        total = jnp.sum(raised, axis=0, keepdims=True)
        out_t = jnp.dot(
            values_t[which * HDIM : (which + 1) * HDIM],
            raised.astype(BF16),
            preferred_element_type=F32,
        )
        parts.append(out_t * (1.0 / total))
        lse_ref[0, 0, which : which + 1, :] = peak + jnp.log(total)
    o_ref[...] = jnp.concatenate(parts, axis=0).T.astype(BF16)


def attn_bwd_kernel(q_ref, k_ref, v_ref, do_ref, lse_ref, dq_ref, dk_ref, dv_ref, dk_acc, dv_acc):
    tile = pl.program_id(1)
    rows = q_ref.shape[0]
    scale = HDIM ** (-0.5)

    @pl.when(tile == 0)
    def _():
        dk_acc[...] = jnp.zeros_like(dk_acc)
        dv_acc[...] = jnp.zeros_like(dv_acc)

    queries = q_ref[...] * jnp.asarray(scale, BF16)
    d_out = do_ref[...]
    keys = k_ref[...]
    values = v_ref[...]
    keys_t = keys.astype(F32).T.astype(BF16)
    parts = []
    for which in range(2):
        mask = head_mask(rows, which)
        q_masked = jnp.where(mask, queries, jnp.zeros_like(queries))
        do_masked = jnp.where(mask, d_out, jnp.zeros_like(d_out))
        scores = nt_dot(keys, q_masked)
        probs = jnp.exp(scores - lse_ref[0, 0, which : which + 1, :])
        d_probs = nt_dot(values, do_masked)
        centre = jnp.sum(probs * d_probs, axis=0, keepdims=True)
        d_scores = (probs * (d_probs - centre)).astype(BF16)
        dv_acc[...] += jnp.dot(probs.astype(BF16), do_masked, preferred_element_type=F32)
        dk_acc[...] += jnp.dot(d_scores, q_masked, preferred_element_type=F32)
        parts.append(
            jnp.dot(
                keys_t[which * HDIM : (which + 1) * HDIM], d_scores, preferred_element_type=F32
            )
        )
    dq_ref[...] = (jnp.concatenate(parts, axis=0).T * scale).astype(BF16)

    @pl.when(tile == pl.num_programs(1) - 1)
    def _():
        dk_ref[...] = dk_acc[...].astype(BF16)
        dv_ref[...] = dv_acc[...].astype(BF16)


def padded_columns(columns):
    return -(-columns // LANES) * LANES


def pad_heads(packed, pieces):
    columns = packed.shape[1] // pieces
    wide = padded_columns(columns)
    if wide == columns:
        return packed
    split = packed.reshape(packed.shape[0], pieces, columns)
    return jnp.pad(split, ((0, 0), (0, 0), (0, wide - columns))).reshape(
        packed.shape[0], pieces * wide
    )


def attention_forward(packed):
    length = packed.shape[0]
    columns = packed.shape[1] // 3
    wide = padded_columns(columns)
    pairs = wide // LANES
    rows, tiles = length, 1
    packed = pad_heads(packed, 3)
    mixed, lse = pl.pallas_call(
        attn_fwd_kernel,
        grid=(pairs, tiles),
        in_specs=[
            pl.BlockSpec((rows, LANES), lambda p, t: (t, p)),
            pl.BlockSpec((length, LANES), lambda p, t: (0, pairs + p)),
            pl.BlockSpec((length, LANES), lambda p, t: (0, 2 * pairs + p)),
        ],
        out_specs=[
            pl.BlockSpec((rows, LANES), lambda p, t: (t, p)),
            pl.BlockSpec((1, 1, 8, rows), lambda p, t: (p, t, 0, 0)),
        ],
        out_shape=[
            jax.ShapeDtypeStruct((length, wide), BF16),
            jax.ShapeDtypeStruct((pairs, tiles, 8, rows), F32),
        ],
        compiler_params=pltpu.CompilerParams(vmem_limit_bytes=40 * 1024 * 1024),
        cost_estimate=pl.CostEstimate(
            flops=8 * length * length * wide,
            bytes_accessed=8 * length * wide,
            transcendentals=length * length * wide // HDIM,
        ),
    )(packed, packed, packed)
    return mixed[:, :columns], lse


def attention_backward(packed, d_mixed, lse):
    length = packed.shape[0]
    columns = packed.shape[1] // 3
    wide = padded_columns(columns)
    pairs = wide // LANES
    rows, tiles = length, 1
    packed = pad_heads(packed, 3)
    d_mixed = pad_heads(d_mixed, 1)
    grads = pl.pallas_call(
        attn_bwd_kernel,
        grid=(pairs, tiles),
        in_specs=[
            pl.BlockSpec((rows, LANES), lambda p, t: (t, p)),
            pl.BlockSpec((length, LANES), lambda p, t: (0, pairs + p)),
            pl.BlockSpec((length, LANES), lambda p, t: (0, 2 * pairs + p)),
            pl.BlockSpec((rows, LANES), lambda p, t: (t, p)),
            pl.BlockSpec((1, 1, 8, rows), lambda p, t: (p, t, 0, 0)),
        ],
        out_specs=[
            pl.BlockSpec((rows, LANES), lambda p, t: (t, p)),
            pl.BlockSpec((length, LANES), lambda p, t: (0, p)),
            pl.BlockSpec((length, LANES), lambda p, t: (0, p)),
        ],
        out_shape=[jax.ShapeDtypeStruct((length, wide), BF16)] * 3,
        scratch_shapes=[pltpu.VMEM((length, LANES), F32)] * 2,
        compiler_params=pltpu.CompilerParams(vmem_limit_bytes=48 * 1024 * 1024),
        cost_estimate=pl.CostEstimate(
            flops=20 * length * length * wide,
            bytes_accessed=14 * length * wide,
            transcendentals=length * length * wide // HDIM,
        ),
    )(packed, packed, packed, d_mixed, lse)
    return jnp.concatenate([part[:, :columns] for part in grads], axis=1)


def normalized(values_in):
    centre = jnp.mean(values_in, axis=-1, keepdims=True)
    offsets = values_in - centre
    spread = jnp.mean(offsets * offsets, axis=-1, keepdims=True)
    factor = lax.rsqrt(spread + EPS)
    return offsets * factor, factor


def modulate(values_in, mod_rows, first):
    normal, _ = normalized(values_in)
    shift = mod_rows[:, first][:, None]
    scale = mod_rows[:, first + 1][:, None]
    return (normal * (1.0 + scale) + shift).astype(BF16)


def modulate_backward(values_in, d_out, mod_rows, first):
    normal, factor = normalized(values_in)
    scale = mod_rows[:, first + 1][:, None]
    d_shift = jnp.sum(d_out, axis=1)
    d_scale = jnp.sum(d_out * normal, axis=1)
    d_normal = d_out * (1.0 + scale)
    mean_plain = jnp.mean(d_normal, axis=-1, keepdims=True)
    mean_along = jnp.mean(d_normal * normal, axis=-1, keepdims=True)
    return (d_normal - mean_plain - normal * mean_along) * factor, d_shift, d_scale


def gelu_tanh(values_in):
    return jax.nn.gelu(values_in, approximate=True)


def tied(values, *others):
    return lax.optimization_barrier((values, *others))


def both(own, other):
    return jnp.concatenate([own, other], axis=0)


def rows_dot(rows, page):
    return dot32("...d,df->...f", rows, page)


def back_dot(rows, page):
    return dot32("...f,df->...d", rows, page)


def back_sum(rows_list, pages):
    return sum(back_dot(rows, page) for rows, page in zip(rows_list, pages))


def flat(values):
    return values.reshape(-1, values.shape[-1])


def row_major(values):
    return with_layout_constraint(values, Layout(major_to_minor=tuple(range(values.ndim))))


def page_grad(left, right):
    grad = lax.dot_general(
        flat(left), flat(right), (((0,), (0,)), ((), ())), preferred_element_type=F32
    )
    return row_major(grad.astype(BF16))


def token_halves(values, seqs):
    return values[:seqs], values[seqs:]


def to_attention(image_parts, text_parts):
    packed = [
        jnp.concatenate([image, text], axis=1) for image, text in zip(image_parts, text_parts)
    ]
    packed = jnp.stack(packed, axis=1)
    return packed.reshape(-1, *packed.shape[2:])


def from_attention(values, blocks, image_rows):
    values = values.reshape(-1, blocks, *values.shape[1:])
    image = [values[:, block, :image_rows] for block in range(blocks)]
    text = [values[:, block, image_rows:] for block in range(blocks)]
    return image, text


def mlp_result(image_act, text_act, down_w, middle, mods):
    other = back_sum(image_act[1], down_w[0]).astype(BF16)
    text_terms = back_dot(text_act, down_w[1][0])
    own = back_sum(image_act[0], down_w[0])
    (mlp,) = sum_over_others(own, other, text_terms)
    return mlp, [middle[u] + mods[u][:, 5][:, None] * mlp[u] for u in range(2)]


def forward_layer(streams, mods, attn_w, mlp_shards, next_shards, early):
    seqs, image_rows = streams[0].shape[:2]
    with jax.named_scope("attention"):
        normed = [modulate(streams[u], mods[u], 0) for u in range(2)]
        image_one, text_one = rows_of_others(*normed)
        image_shards = jnp.concatenate([mlp_shards[0], *next_shards[:1]], axis=0)
        mlp_shards = jnp.concatenate(mlp_shards, axis=0)
        text_one, mlp_shards, image_shards = tied(text_one, mlp_shards, image_shards)
        mlp_w = [gather_pages(mlp_shards)]
        others = with_blocks(image_shards)[1:]
        qkv_w, out_w = attention_pages(attn_w)
        blocks = len(qkv_w[0])
        text_heads = rows_dot(text_one, qkv_w[1][0]).astype(BF16)
        text_heads = to_sequences(text_heads, blocks)
        image_heads = [
            both(*[rows_dot(part, page).astype(BF16) for part in image_one]) for page in qkv_w[0]
        ]
        packed = to_attention(image_heads, text_heads)
        tokens, columns = packed.shape[1:]
        if early:
            early, packed = tied(early, packed)
            early = rows_of_others(*early)
        packed = lax.all_to_all(packed, "dp", 0, 0, tiled=True)
        packed = packed.reshape(-1, columns)
        mixed, lse = attention_forward(packed)
        mixed = mixed.reshape(-1, tokens, columns // 3)
        mixed = lax.all_to_all(mixed, "dp", 0, 0, tiled=True)
        mixed, others, early = tied(mixed, others, early)
        image_mixed, text_mixed = from_attention(mixed, blocks, image_rows)
        text_mixed = to_blocks(text_mixed, seqs)
        other = back_sum([part[seqs:] for part in image_mixed], out_w[0])
        text_terms = back_dot(text_mixed, out_w[1][0])
        own = back_sum([part[:seqs] for part in image_mixed], out_w[0])
        others, mlp_w[0], own = tied(others, mlp_w[0], own)
        mlp_w.append(gather_pages(jnp.concatenate([part[:2] for part in others], axis=0)))
        next_others = [part[2:] for part in others]
        (attn,) = sum_over_others(own, other, text_terms)
    with jax.named_scope("mlp"):
        middle = [streams[u] + mods[u][:, 2][:, None] * attn[u] for u in range(2)]
        normed_two = [modulate(middle[u], mods[u], 3) for u in range(2)]
        image_two, text_two = rows_of_others(*normed_two)
        up_w, down_w = mlp_pages(mlp_w)
        image_up = [[rows_dot(part, page) for page in up_w[0]] for part in image_two]
        next_attn = None
        if next_shards:
            image_up[1][0], mlp_w[1], next_shards, next_others = tied(
                image_up[1][0], mlp_w[1], next_shards, next_others
            )
            next_attn = (gather_pages(jnp.concatenate([*next_shards, *next_others], axis=0)),)
        image_act = [[gelu_tanh(up).astype(BF16) for up in part] for part in image_up]
        text_up = rows_dot(text_two, up_w[1][0])
        text_act = gelu_tanh(text_up).astype(BF16)
        mlp = result = None
        if not early:
            mlp, result = mlp_result(image_act, text_act, down_w, middle, mods)
    saved = dict(
        streams=streams,
        image_one=both(*image_one),
        text_one=text_one,
        packed=packed,
        lse=lse,
        image_mixed=image_mixed,
        text_mixed=text_mixed,
        attn=attn,
        middle=middle,
        image_two=both(*image_two),
        text_two=text_two,
        image_up=image_up,
        image_act=image_act,
        text_up=text_up,
        text_act=text_act,
        mlp=mlp,
    )
    return result, saved, (attn_w, mlp_w), next_attn, early


def gelu_pull(up_values, d_active):
    return jax.vjp(gelu_tanh, up_values)[1](d_active)[0].astype(BF16)


def scatter_pages(wide):
    return lax.psum_scatter(wide, "dp", scatter_dimension=0, tiled=True)


def send_blocks(slab, blocks):
    width = slab.shape[1] // (blocks + 1)
    parts = [slab[:, (block + 1) * width : (block + 2) * width] for block in range(1, blocks)]
    return [slab[:, : 2 * width]] + [hi_swap(part, at + 1) for at, part in enumerate(parts)]


def shard_rows(parts):
    width = parts[0].shape[1] // 2
    image = parts[0][:, :width].astype(F32)
    for part in parts[1:]:
        image = image + part.astype(F32)
    return image, parts[0][:, width:].astype(F32)


def page_list(image_first, image_second, text_first, text_second):
    pages = [image_first[0], image_second[0], text_first, text_second]
    for pair in zip(image_first[1:], image_second[1:]):
        pages += pair
    return pages


def mlp_shard(parts):
    rows = shard_rows(parts)
    half = rows[0].shape[1] // 2
    return (
        jnp.stack([part[:, half:] for part in rows]),
        jnp.stack([part[:, :half].T for part in rows]),
    )


def attention_shard(parts):
    rows = shard_rows(parts)
    columns = rows[0].shape[1] // 4
    return (
        jnp.stack(
            [
                jnp.stack([part[:, at * columns : (at + 1) * columns] for at in range(3)])
                for part in rows
            ]
        ),
        jnp.stack([part[:, 3 * columns :].T for part in rows]),
    )


def gated_rows(rows, mods, gate):
    return [(mods[u][:, gate][:, None] * rows[u]).astype(BF16) for u in range(2)]


def backward_layer(grads_out, mods, weights, saved, pending, final, dmlp):
    seqs, image_rows = grads_out[0].shape[:2]
    qkv_w, out_w = attention_pages(weights[0])
    up_w, down_w = mlp_pages(weights[1])
    blocks = len(qkv_w[0])
    middle, attn, mlp = saved["middle"], saved["attn"], saved["mlp"]
    with jax.named_scope("mlp_grad"):
        image_dmlp, text_dmlp = dmlp or rows_of_others(*gated_rows(grads_out, mods, 5))
        image_dup = [
            [
                gelu_pull(saved["image_up"][at][block], rows_dot(image_dmlp[at], down_w[0][block]))
                for block in range(blocks)
            ]
            for at in range(2)
        ]
        other = back_sum(image_dup[1], up_w[0])
        text_dup = gelu_pull(saved["text_up"], rows_dot(text_dmlp, down_w[1][0]))
        text_terms = back_dot(text_dup, up_w[1][0])
        own = back_sum(image_dup[0], up_w[0])
        dmlp_rows = both(*image_dmlp)
        grads = page_list(
            [page_grad(dmlp_rows, both(*parts)) for parts in zip(*saved["image_act"])],
            [page_grad(saved["image_two"], both(*parts)) for parts in zip(*image_dup)],
            page_grad(text_dmlp, saved["text_act"]),
            page_grad(saved["text_two"], text_dup),
        )
        wide = jnp.concatenate(grads, axis=1)
        d_two, wide = sum_over_others(own, other, text_terms, wide)
        mlp_slab = scatter_pages(wide)
        d_middle, d_shift_two, d_scale_two = [], [], []
        for u in range(2):
            d_values, d_shift, d_scale = modulate_backward(middle[u], d_two[u], mods[u], 3)
            d_middle.append(grads_out[u] + d_values)
            d_shift_two.append(d_shift)
            d_scale_two.append(d_scale)
    with jax.named_scope("attention_grad"):
        image_dattn, text_dattn = rows_of_others(*gated_rows(d_middle, mods, 2))
        d_gate_one = [jnp.sum(d_middle[u] * attn[u], axis=1) for u in range(2)]
        text_dmixed = to_sequences(rows_dot(text_dattn, out_w[1][0]).astype(BF16), blocks)
        image_dmixed = [
            both(*[rows_dot(part, page).astype(BF16) for part in image_dattn]) for page in out_w[0]
        ]
        d_mixed = to_attention(image_dmixed, text_dmixed)
        tokens, columns = d_mixed.shape[1:]
        result = None
        if mlp is None:
            late, d_mixed = tied((saved["image_act"], saved["text_act"]), d_mixed)
            mlp, result = mlp_result(*late, down_w, middle, mods)
        d_mixed = lax.all_to_all(d_mixed, "dp", 0, 0, tiled=True)
        done = []
        if pending:
            mlp_before, d_mixed = tied(pending[0], d_mixed)
            done.append(mlp_shard(send_blocks(mlp_before, blocks)))
        d_mixed = d_mixed.reshape(-1, columns)
        d_packed = attention_backward(saved["packed"], d_mixed, saved["lse"])
        if pending:
            attn_before, d_packed = tied(pending[1], d_packed)
            attn_before = send_blocks(attn_before, blocks)
        d_packed = d_packed.reshape(-1, tokens, 3 * columns)
        d_packed = lax.all_to_all(d_packed, "dp", 0, 0, tiled=True)
        if pending:
            done[0], attn_before, d_packed = tied(done[0], attn_before, d_packed)
            done.append(attention_shard(attn_before))
        if result:
            mlp, result, d_packed = tied(mlp, result, d_packed)
        d_gate_two = [jnp.sum(grads_out[u] * mlp[u], axis=1) for u in range(2)]
        image_dproj, text_dproj = from_attention(d_packed, blocks, image_rows)
        text_dproj = to_blocks(text_dproj, seqs)
        grad_rows = image_dproj
        if not final:
            other = back_sum([part[seqs:] for part in image_dproj], qkv_w[0]).astype(BF16)
            grad_rows, other = tied(image_dproj, other)
        dattn_rows = both(*image_dattn)
        grads = page_list(
            [page_grad(saved["image_one"], part) for part in grad_rows],
            [page_grad(dattn_rows, part) for part in saved["image_mixed"]],
            page_grad(saved["text_one"], text_dproj),
            page_grad(text_dattn, saved["text_mixed"]),
        )
        wide = jnp.concatenate(grads, axis=1)
        if final:
            wide, image_dproj = tied(wide, image_dproj)
            other = back_sum([part[seqs:] for part in image_dproj], qkv_w[0]).astype(BF16)
        text_terms = back_dot(text_dproj, qkv_w[1][0])
        own = back_sum([part[:seqs] for part in image_dproj], qkv_w[0])
        (d_one,) = sum_over_others(own, other, text_terms)
        wide, mlp_slab = tied(wide, mlp_slab)
        attn_slab = scatter_pages(wide)
        d_inputs, d_mods = [], []
        for u in range(2):
            d_values, d_shift, d_scale = modulate_backward(
                saved["streams"][u], d_one[u], mods[u], 0
            )
            d_inputs.append(d_middle[u] + d_values)
            d_mods.append(
                jnp.concatenate(
                    [d_shift, d_scale, d_gate_one[u], d_shift_two[u], d_scale_two[u], d_gate_two[u]],
                    axis=1,
                )
            )
    return d_inputs, jnp.concatenate(d_mods), (mlp_slab, attn_slab), done, result


def with_blocks(pages):
    hi_count = lax.axis_size("tensor") // 2
    return [pages] + [hi_swap(pages, block) for block in range(1, hi_count)]


def gather_pages(pages):
    return lax.all_gather(pages, "dp", axis=1, tiled=True)


def attn_page(w_qkv, w_out, layer_at, u):
    qkv = w_qkv[layer_at, u].transpose(1, 0, 2)
    qkv = qkv.reshape(qkv.shape[0], -1)
    return jnp.concatenate([qkv, w_out[layer_at, u].T], axis=1)


def attention_shards(w_qkv, w_out, layer_at):
    return [attn_page(w_qkv, w_out, layer_at, u)[None] for u in range(2)]


def mlp_shards(w_up, w_down, layer_at):
    return [jnp.stack([w_up[layer_at, u], w_down[layer_at, u].T]) for u in range(2)]


def attention_pages(gathered):
    pages = [pages[at] for pages in gathered for at in range(pages.shape[0])]
    qkv_columns = pages[0].shape[1] * 3 // 4
    by_stream = [[pages[0], *pages[2:]], [pages[1]]]
    qkv_w = [[page[:, :qkv_columns] for page in group] for group in by_stream]
    out_w = [[page[:, qkv_columns:] for page in group] for group in by_stream]
    return qkv_w, out_w


def mlp_pages(gathered):
    pages = [pages[at] for pages in gathered for at in range(pages.shape[0])]
    by_stream = [[*pages[:2], *pages[4:]], pages[2:4]]
    return [group[0::2] for group in by_stream], [group[1::2] for group in by_stream]


def per_device(
    image_in,
    text_in,
    cond_table,
    cond_index,
    w_mod,
    w_qkv,
    w_out,
    w_up,
    w_down,
    cot_image,
    cot_text,
):
    n_tensor = lax.axis_size("tensor")
    dp_at = lax.axis_index("dp")
    micro_count, own_rows = image_in.shape[:2]
    seqs = micro_count * own_rows
    model_width = image_in.shape[3]
    layer_count = w_qkv.shape[0]
    slab_rows = w_mod.shape[2]
    column_count = w_mod.shape[3]
    index_flat = cond_index.reshape(-1)
    attn_shards = [attention_shards(w_qkv, w_out, at) for at in range(layer_count)]
    all_mlp_shards = [mlp_shards(w_up, w_down, at) for at in range(layer_count)]
    first_attn = gather_pages(jnp.concatenate(attn_shards[0], axis=0))
    with jax.named_scope("modulation"):
        onehot = (
            index_flat[:, None] == jnp.arange(cond_table.shape[0], dtype=jnp.int32)[None, :]
        ).astype(F32)
        cond_slab = lax.dynamic_slice_in_dim(cond_table, dp_at * slab_rows, slab_rows, 1)
        cond_slab = jnp.dot(onehot, cond_slab, precision=HIGHEST, preferred_element_type=F32)
        silu_slab = jax.nn.silu(cond_slab).astype(BF16)
        partial_mod = dot32("sd,lmdc->lmsc", silu_slab, w_mod)
        partial_mod = partial_mod.reshape(
            layer_count * 2, micro_count, n_tensor, own_rows * column_count
        )
        partial_mod = partial_mod.transpose(2, 0, 1, 3).reshape(n_tensor, -1, column_count)
        partial_mod = lax.all_to_all(partial_mod, "tensor", 0, 0, tiled=True)
        attn_own, partial_mod = tied(attn_shards[0], partial_mod)
        attn_others = with_blocks(attn_own[0])[1:]
        partial_mod = axis_sum(partial_mod, "dp")
        mod_own = partial_mod.transpose(1, 0, 2)
        mod_own = mod_own.reshape(layer_count, 2, seqs, 6, model_width)
    rest, first_attn, mod_own = tied(attn_others, first_attn, mod_own)
    attn_w = (first_attn, gather_pages(jnp.concatenate(rest, axis=0)))
    mods = [[mod_own[layer_at, u] for u in range(2)] for layer_at in range(layer_count)]

    def rows_in(values):
        return values.reshape(seqs, values.shape[2], model_width).astype(F32)

    def rows_out(values):
        return values.reshape(micro_count, own_rows, values.shape[1], model_width)

    streams = [rows_in(image_in), rows_in(text_in)]
    grads_now = [rows_in(cot_image), rows_in(cot_text)]
    saved, weights = [], []
    for layer_at in range(layer_count):
        last = layer_at + 1 == layer_count
        streams, kept, gathered, attn_w, dmlp = forward_layer(
            streams,
            mods[layer_at],
            attn_w,
            all_mlp_shards[layer_at],
            [] if last else attn_shards[layer_at + 1],
            gated_rows(grads_now, mods[layer_at], 5) if last else (),
        )
        weights.append(gathered)
        saved.append(kept)
    shards = [None] * layer_count
    d_mods = [None] * layer_count
    pending = None
    for layer_at in reversed(range(layer_count)):
        grads_now, d_mods[layer_at], slabs, done, result = backward_layer(
            grads_now,
            mods[layer_at],
            weights[layer_at],
            saved[layer_at],
            pending,
            layer_at == 0,
            dmlp,
        )
        dmlp = None
        streams = result or streams
        if pending:
            shards[layer_at + 1] = done
        pending = slabs
    with jax.named_scope("modulation_grad"):
        d_mods = jnp.concatenate(d_mods).reshape(layer_count * 2 * seqs, n_tensor, column_count)
        d_mods = lax.all_to_all(d_mods.transpose(1, 0, 2), "tensor", 0, 0, tiled=True)
        blocks = n_tensor // 2
        mlp_parts = send_blocks(pending[0], blocks)
        mlp_parts, attn_slab = tied(mlp_parts, pending[1])
        attn_parts = send_blocks(attn_slab, blocks)
        d_mods = axis_sum(d_mods, "dp")
        d_mods = d_mods.reshape(n_tensor, layer_count, 2, micro_count, own_rows, column_count)
        d_columns = d_mods.transpose(1, 2, 3, 0, 4, 5)
        d_columns = d_columns.reshape(layer_count, 2, -1, column_count)
        grad_w_mod = jnp.einsum(
            "sd,lmsc->lmdc",
            silu_slab.astype(F32),
            d_columns,
            precision=HIGHEST,
            preferred_element_type=F32,
        )
        d_silu = jnp.einsum(
            "lmsc,lmdc->sd",
            d_columns,
            w_mod.astype(F32),
            precision=HIGHEST,
            preferred_element_type=F32,
        )
    with jax.named_scope("conditioning_grad"):
        d_cond = jax.vjp(jax.nn.silu, cond_slab)[1](d_silu)[0]
        grad_cond = axis_sum(
            jnp.dot(onehot.T, d_cond, precision=HIGHEST, preferred_element_type=F32), "tensor"
        )
    with jax.named_scope("weight_grads"):
        mlp_done = [mlp_shard(mlp_parts)] + [layer[0] for layer in shards[1:]]
        grad_up, grad_down = [jnp.stack(parts) for parts in zip(*mlp_done)]
        attn_parts, grad_up, grad_down, grad_w_mod, grad_cond = tied(
            attn_parts, grad_up, grad_down, grad_w_mod, grad_cond
        )
        attn_done = [attention_shard(attn_parts)] + [layer[1] for layer in shards[1:]]
        grad_qkv, grad_out = [jnp.stack(parts) for parts in zip(*attn_done)]
    return (
        rows_out(streams[0].astype(BF16)),
        rows_out(streams[1].astype(BF16)),
        rows_out(grads_now[0]),
        rows_out(grads_now[1]),
        grad_cond,
        grad_w_mod,
        grad_qkv,
        grad_out,
        grad_up,
        grad_down,
    )


def solution(mesh):
    rows = P(None, "tensor", "dp", None)
    up_like = P(None, None, "dp", "tensor")
    down_like = P(None, None, "tensor", "dp")
    qkv_like = P(None, None, None, "dp", "tensor")
    return jax.shard_map(
        per_device,
        mesh=mesh,
        in_specs=(
            rows,
            rows,
            P(),
            P(),
            up_like,
            qkv_like,
            down_like,
            up_like,
            down_like,
            rows,
            rows,
        ),
        out_specs=(
            rows,
            rows,
            rows,
            rows,
            P(None, "dp"),
            up_like,
            qkv_like,
            down_like,
            up_like,
            down_like,
        ),
        check_vma=False,
    )
```

```python
import functools

import jax
import jax.numpy as jnp
from jax import lax
from jax.experimental import pallas as pl
from jax.experimental.layout import Layout, with_layout_constraint
from jax.experimental.pallas import tpu as pltpu
from jax.sharding import PartitionSpec as P

HDIM = 64
LANES = 128
EPS = 1e-06
HIGHEST = lax.Precision.HIGHEST
BF16 = jnp.bfloat16
F32 = jnp.float32


def dot32(pattern, left, right):
    return jnp.einsum(pattern, left, right, preferred_element_type=F32)


def tensor_swap(values, distance):
    count = lax.axis_size("tensor")
    return lax.ppermute(values, "tensor", [(i, i ^ distance) for i in range(count)])


def pair_swap(values):
    return tensor_swap(values, 1)


def hi_swap(values, block):
    return tensor_swap(values, 2 * block)


def axis_sum(values, axis):
    count = lax.axis_size(axis)
    step = 1
    while step < count:
        values = values + lax.ppermute(values, axis, [(i, i ^ step) for i in range(count)])
        step *= 2
    return values


def rows_of_others(image, text):
    image_rows = image.shape[1]
    image, text = tied(image, text)
    received = pair_swap(jnp.concatenate([image, text], axis=1))
    far = [tensor_swap(text, at) for at in range(2, lax.axis_size("tensor"))]
    return (image, received[:, :image_rows]), jnp.stack([text, received[:, image_rows:], *far])


def sum_over_others(image_own, image_other, text_terms, *meanwhile):
    image_rows = image_own.shape[1]
    sent = jnp.concatenate([image_other.astype(BF16), text_terms[1].astype(BF16)], axis=1)
    received = pair_swap(sent)
    far = [
        tensor_swap(text_terms[at].astype(BF16), at) for at in range(2, text_terms.shape[0])
    ]
    received, far, *meanwhile = tied(received, far, *meanwhile)
    image = image_own + received[:, :image_rows].astype(F32)
    text = text_terms[0] + received[:, image_rows:].astype(F32)
    for part in far:
        text = text + part.astype(F32)
    return [image, text], *meanwhile


def to_sequences(parts, blocks):
    received = [parts[:2]] + [
        hi_swap(parts[2 * block : 2 * block + 2], block) for block in range(1, blocks)
    ]
    return [flat_pairs(part) for part in received]


def to_blocks(by_block, seqs):
    split = [part.reshape(2, seqs, *part.shape[1:]) for part in by_block]
    parts = [split[0]] + [hi_swap(split[block], block) for block in range(1, len(split))]
    return jnp.concatenate(parts, axis=0)


def flat_pairs(values):
    return values.reshape(-1, *values.shape[2:])


def head_mask(rows, which):
    lane = lax.broadcasted_iota(jnp.int32, (rows, LANES), 1)
    return (lane < HDIM) if which == 0 else (lane >= HDIM)


def nt_dot(left, right):
    return lax.dot_general(left, right, (((1,), (1,)), ((), ())), preferred_element_type=F32)


def attn_fwd_kernel(q_ref, k_ref, v_ref, o_ref, lse_ref):
    rows = q_ref.shape[0]
    queries = q_ref[...] * jnp.asarray(HDIM ** (-0.5), BF16)
    keys = k_ref[...]
    values_t = v_ref[...].astype(F32).T.astype(BF16)
    parts = []
    for which in range(2):
        masked = jnp.where(head_mask(rows, which), queries, jnp.zeros_like(queries))
        scores = nt_dot(keys, masked)
        peak = jnp.max(scores, axis=0, keepdims=True)
        raised = jnp.exp(scores - peak)
        total = jnp.sum(raised, axis=0, keepdims=True)
        out_t = jnp.dot(
            values_t[which * HDIM : (which + 1) * HDIM],
            raised.astype(BF16),
            preferred_element_type=F32,
        )
        parts.append(out_t * (1.0 / total))
        lse_ref[0, 0, which : which + 1, :] = peak + jnp.log(total)
    o_ref[...] = jnp.concatenate(parts, axis=0).T.astype(BF16)


def attn_bwd_kernel(q_ref, k_ref, v_ref, do_ref, lse_ref, dq_ref, dk_ref, dv_ref, dk_acc, dv_acc):
    tile = pl.program_id(1)
    rows = q_ref.shape[0]
    scale = HDIM ** (-0.5)

    @pl.when(tile == 0)
    def _():
        dk_acc[...] = jnp.zeros_like(dk_acc)
        dv_acc[...] = jnp.zeros_like(dv_acc)

    queries = q_ref[...] * jnp.asarray(scale, BF16)
    d_out = do_ref[...]
    keys = k_ref[...]
    values = v_ref[...]
    keys_t = keys.astype(F32).T.astype(BF16)
    parts = []
    for which in range(2):
        mask = head_mask(rows, which)
        q_masked = jnp.where(mask, queries, jnp.zeros_like(queries))
        do_masked = jnp.where(mask, d_out, jnp.zeros_like(d_out))
        scores = nt_dot(keys, q_masked)
        probs = jnp.exp(scores - lse_ref[0, 0, which : which + 1, :])
        d_probs = nt_dot(values, do_masked)
        centre = jnp.sum(probs * d_probs, axis=0, keepdims=True)
        d_scores = (probs * (d_probs - centre)).astype(BF16)
        dv_acc[...] += jnp.dot(probs.astype(BF16), do_masked, preferred_element_type=F32)
        dk_acc[...] += jnp.dot(d_scores, q_masked, preferred_element_type=F32)
        parts.append(
            jnp.dot(
                keys_t[which * HDIM : (which + 1) * HDIM], d_scores, preferred_element_type=F32
            )
        )
    dq_ref[...] = (jnp.concatenate(parts, axis=0).T * scale).astype(BF16)

    @pl.when(tile == pl.num_programs(1) - 1)
    def _():
        dk_ref[...] = dk_acc[...].astype(BF16)
        dv_ref[...] = dv_acc[...].astype(BF16)


def padded_columns(columns):
    return -(-columns // LANES) * LANES


def pad_heads(packed, pieces):
    columns = packed.shape[1] // pieces
    wide = padded_columns(columns)
    if wide == columns:
        return packed
    split = packed.reshape(packed.shape[0], pieces, columns)
    return jnp.pad(split, ((0, 0), (0, 0), (0, wide - columns))).reshape(
        packed.shape[0], pieces * wide
    )


def attention_forward(packed):
    length = packed.shape[0]
    columns = packed.shape[1] // 3
    wide = padded_columns(columns)
    pairs = wide // LANES
    rows, tiles = length, 1
    packed = pad_heads(packed, 3)
    mixed, lse = pl.pallas_call(
        attn_fwd_kernel,
        grid=(pairs, tiles),
        in_specs=[
            pl.BlockSpec((rows, LANES), lambda p, t: (t, p)),
            pl.BlockSpec((length, LANES), lambda p, t: (0, pairs + p)),
            pl.BlockSpec((length, LANES), lambda p, t: (0, 2 * pairs + p)),
        ],
        out_specs=[
            pl.BlockSpec((rows, LANES), lambda p, t: (t, p)),
            pl.BlockSpec((1, 1, 8, rows), lambda p, t: (p, t, 0, 0)),
        ],
        out_shape=[
            jax.ShapeDtypeStruct((length, wide), BF16),
            jax.ShapeDtypeStruct((pairs, tiles, 8, rows), F32),
        ],
        compiler_params=pltpu.CompilerParams(vmem_limit_bytes=40 * 1024 * 1024),
        cost_estimate=pl.CostEstimate(
            flops=8 * length * length * wide,
            bytes_accessed=8 * length * wide,
            transcendentals=length * length * wide // HDIM,
        ),
    )(packed, packed, packed)
    return mixed[:, :columns], lse


def attention_backward(packed, d_mixed, lse):
    length = packed.shape[0]
    columns = packed.shape[1] // 3
    wide = padded_columns(columns)
    pairs = wide // LANES
    rows, tiles = length, 1
    packed = pad_heads(packed, 3)
    d_mixed = pad_heads(d_mixed, 1)
    grads = pl.pallas_call(
        attn_bwd_kernel,
        grid=(pairs, tiles),
        in_specs=[
            pl.BlockSpec((rows, LANES), lambda p, t: (t, p)),
            pl.BlockSpec((length, LANES), lambda p, t: (0, pairs + p)),
            pl.BlockSpec((length, LANES), lambda p, t: (0, 2 * pairs + p)),
            pl.BlockSpec((rows, LANES), lambda p, t: (t, p)),
            pl.BlockSpec((1, 1, 8, rows), lambda p, t: (p, t, 0, 0)),
        ],
        out_specs=[
            pl.BlockSpec((rows, LANES), lambda p, t: (t, p)),
            pl.BlockSpec((length, LANES), lambda p, t: (0, p)),
            pl.BlockSpec((length, LANES), lambda p, t: (0, p)),
        ],
        out_shape=[jax.ShapeDtypeStruct((length, wide), BF16)] * 3,
        scratch_shapes=[pltpu.VMEM((length, LANES), F32)] * 2,
        compiler_params=pltpu.CompilerParams(vmem_limit_bytes=48 * 1024 * 1024),
        cost_estimate=pl.CostEstimate(
            flops=20 * length * length * wide,
            bytes_accessed=14 * length * wide,
            transcendentals=length * length * wide // HDIM,
        ),
    )(packed, packed, packed, d_mixed, lse)
    return jnp.concatenate([part[:, :columns] for part in grads], axis=1)


def normalized(values_in):
    centre = jnp.mean(values_in, axis=-1, keepdims=True)
    offsets = values_in - centre
    spread = jnp.mean(offsets * offsets, axis=-1, keepdims=True)
    factor = lax.rsqrt(spread + EPS)
    return offsets * factor, factor


def modulate(values_in, mod_rows, first):
    normal, _ = normalized(values_in)
    shift = mod_rows[:, first][:, None]
    scale = mod_rows[:, first + 1][:, None]
    return (normal * (1.0 + scale) + shift).astype(BF16)


def modulate_backward(values_in, d_out, mod_rows, first):
    normal, factor = normalized(values_in)
    scale = mod_rows[:, first + 1][:, None]
    d_shift = jnp.sum(d_out, axis=1)
    d_scale = jnp.sum(d_out * normal, axis=1)
    d_normal = d_out * (1.0 + scale)
    mean_plain = jnp.mean(d_normal, axis=-1, keepdims=True)
    mean_along = jnp.mean(d_normal * normal, axis=-1, keepdims=True)
    return (d_normal - mean_plain - normal * mean_along) * factor, d_shift, d_scale


def gelu_tanh(values_in):
    return jax.nn.gelu(values_in, approximate=True)


def tied(values, *others):
    return lax.optimization_barrier((values, *others))


def both(own, other):
    return jnp.concatenate([own, other], axis=0)


def rows_dot(rows, page):
    return dot32("...d,df->...f", rows, page)


def back_dot(rows, page):
    return dot32("...f,df->...d", rows, page)


def back_sum(rows_list, pages):
    return sum(back_dot(rows, page) for rows, page in zip(rows_list, pages))


def flat(values):
    return values.reshape(-1, values.shape[-1])


def row_major(values):
    return with_layout_constraint(values, Layout(major_to_minor=tuple(range(values.ndim))))


def page_grad(left, right):
    grad = lax.dot_general(
        flat(left), flat(right), (((0,), (0,)), ((), ())), preferred_element_type=F32
    )
    return row_major(grad.astype(BF16))


def token_halves(values, seqs):
    return values[:seqs], values[seqs:]


def to_attention(image_parts, text_parts):
    packed = [
        jnp.concatenate([image, text], axis=1) for image, text in zip(image_parts, text_parts)
    ]
    packed = jnp.stack(packed, axis=1)
    return packed.reshape(-1, *packed.shape[2:])


def from_attention(values, blocks, image_rows):
    values = values.reshape(-1, blocks, *values.shape[1:])
    image = [values[:, block, :image_rows] for block in range(blocks)]
    text = [values[:, block, image_rows:] for block in range(blocks)]
    return image, text


def mlp_result(image_act, text_act, down_w, middle, mods):
    other = back_sum(image_act[1], down_w[0]).astype(BF16)
    text_terms = back_dot(text_act, down_w[1][0])
    own = back_sum(image_act[0], down_w[0])
    (mlp,) = sum_over_others(own, other, text_terms)
    return mlp, [middle[u] + mods[u][:, 5][:, None] * mlp[u] for u in range(2)]


def forward_layer(streams, mods, attn_w, mlp_shards, next_shards, early):
    seqs, image_rows = streams[0].shape[:2]
    with jax.named_scope("attention"):
        normed = [modulate(streams[u], mods[u], 0) for u in range(2)]
        image_one, text_one = rows_of_others(*normed)
        image_shards = jnp.concatenate([mlp_shards[0], *next_shards[:1]], axis=0)
        mlp_shards = jnp.concatenate(mlp_shards, axis=0)
        text_one, mlp_shards, image_shards = tied(text_one, mlp_shards, image_shards)
        mlp_w = [gather_pages(mlp_shards)]
        others = with_blocks(image_shards)[1:]
        qkv_w, out_w = attention_pages(attn_w)
        blocks = len(qkv_w[0])
        text_heads = rows_dot(text_one, qkv_w[1][0]).astype(BF16)
        text_heads = to_sequences(text_heads, blocks)
        image_heads = [
            both(*[rows_dot(part, page).astype(BF16) for part in image_one]) for page in qkv_w[0]
        ]
        packed = to_attention(image_heads, text_heads)
        tokens, columns = packed.shape[1:]
        if early:
            early, packed = tied(early, packed)
            early = rows_of_others(*early)
        packed = lax.all_to_all(packed, "dp", 0, 0, tiled=True)
        packed = packed.reshape(-1, columns)
        mixed, lse = attention_forward(packed)
        mixed = mixed.reshape(-1, tokens, columns // 3)
        mixed = lax.all_to_all(mixed, "dp", 0, 0, tiled=True)
        mixed, others, early = tied(mixed, others, early)
        image_mixed, text_mixed = from_attention(mixed, blocks, image_rows)
        text_mixed = to_blocks(text_mixed, seqs)
        other = back_sum([part[seqs:] for part in image_mixed], out_w[0])
        text_terms = back_dot(text_mixed, out_w[1][0])
        own = back_sum([part[:seqs] for part in image_mixed], out_w[0])
        others, mlp_w[0], own = tied(others, mlp_w[0], own)
        mlp_w.append(gather_pages(jnp.concatenate([part[:2] for part in others], axis=0)))
        next_others = [part[2:] for part in others]
        (attn,) = sum_over_others(own, other, text_terms)
    with jax.named_scope("mlp"):
        middle = [streams[u] + mods[u][:, 2][:, None] * attn[u] for u in range(2)]
        normed_two = [modulate(middle[u], mods[u], 3) for u in range(2)]
        image_two, text_two = rows_of_others(*normed_two)
        up_w, down_w = mlp_pages(mlp_w)
        image_up = [[rows_dot(part, page) for page in up_w[0]] for part in image_two]
        next_attn = None
        if next_shards:
            image_up[1][0], mlp_w[1], next_shards, next_others = tied(
                image_up[1][0], mlp_w[1], next_shards, next_others
            )
            next_attn = (gather_pages(jnp.concatenate([*next_shards, *next_others], axis=0)),)
        image_act = [[gelu_tanh(up).astype(BF16) for up in part] for part in image_up]
        text_up = rows_dot(text_two, up_w[1][0])
        text_act = gelu_tanh(text_up).astype(BF16)
        mlp = result = None
        if not early:
            mlp, result = mlp_result(image_act, text_act, down_w, middle, mods)
    saved = dict(
        streams=streams,
        image_one=both(*image_one),
        text_one=text_one,
        packed=packed,
        lse=lse,
        image_mixed=image_mixed,
        text_mixed=text_mixed,
        attn=attn,
        middle=middle,
        image_two=both(*image_two),
        text_two=text_two,
        image_up=image_up,
        image_act=image_act,
        text_up=text_up,
        text_act=text_act,
        mlp=mlp,
    )
    return result, saved, (attn_w, mlp_w), next_attn, early


def gelu_pull(up_values, d_active):
    return jax.vjp(gelu_tanh, up_values)[1](d_active)[0].astype(BF16)


def scatter_pages(wide):
    return lax.psum_scatter(wide, "dp", scatter_dimension=0, tiled=True)


def send_blocks(slab, blocks):
    width = slab.shape[1] // (blocks + 1)
    parts = [slab[:, (block + 1) * width : (block + 2) * width] for block in range(1, blocks)]
    return [slab[:, : 2 * width]] + [hi_swap(part, at + 1) for at, part in enumerate(parts)]


def shard_rows(parts):
    width = parts[0].shape[1] // 2
    image = parts[0][:, :width].astype(F32)
    for part in parts[1:]:
        image = image + part.astype(F32)
    return image, parts[0][:, width:].astype(F32)


def page_list(image_first, image_second, text_first, text_second):
    pages = [image_first[0], image_second[0], text_first, text_second]
    for pair in zip(image_first[1:], image_second[1:]):
        pages += pair
    return pages


def mlp_shard(parts):
    rows = shard_rows(parts)
    half = rows[0].shape[1] // 2
    return (
        jnp.stack([part[:, half:] for part in rows]),
        jnp.stack([part[:, :half].T for part in rows]),
    )


def attention_shard(parts):
    rows = shard_rows(parts)
    columns = rows[0].shape[1] // 4
    return (
        jnp.stack(
            [
                jnp.stack([part[:, at * columns : (at + 1) * columns] for at in range(3)])
                for part in rows
            ]
        ),
        jnp.stack([part[:, 3 * columns :].T for part in rows]),
    )


def gated_rows(rows, mods, gate):
    return [(mods[u][:, gate][:, None] * rows[u]).astype(BF16) for u in range(2)]


def backward_layer(grads_out, mods, weights, saved, pending, final, dmlp):
    seqs, image_rows = grads_out[0].shape[:2]
    qkv_w, out_w = attention_pages(weights[0])
    up_w, down_w = mlp_pages(weights[1])
    blocks = len(qkv_w[0])
    middle, attn, mlp = saved["middle"], saved["attn"], saved["mlp"]
    with jax.named_scope("mlp_grad"):
        image_dmlp, text_dmlp = dmlp or rows_of_others(*gated_rows(grads_out, mods, 5))
        image_dup = [
            [
                gelu_pull(saved["image_up"][at][block], rows_dot(image_dmlp[at], down_w[0][block]))
                for block in range(blocks)
            ]
            for at in range(2)
        ]
        other = back_sum(image_dup[1], up_w[0])
        text_dup = gelu_pull(saved["text_up"], rows_dot(text_dmlp, down_w[1][0]))
        text_terms = back_dot(text_dup, up_w[1][0])
        own = back_sum(image_dup[0], up_w[0])
        dmlp_rows = both(*image_dmlp)
        grads = page_list(
            [page_grad(dmlp_rows, both(*parts)) for parts in zip(*saved["image_act"])],
            [page_grad(saved["image_two"], both(*parts)) for parts in zip(*image_dup)],
            page_grad(text_dmlp, saved["text_act"]),
            page_grad(saved["text_two"], text_dup),
        )
        wide = jnp.concatenate(grads, axis=1)
        d_two, wide = sum_over_others(own, other, text_terms, wide)
        mlp_slab = scatter_pages(wide)
        d_middle, d_shift_two, d_scale_two = [], [], []
        for u in range(2):
            d_values, d_shift, d_scale = modulate_backward(middle[u], d_two[u], mods[u], 3)
            d_middle.append(grads_out[u] + d_values)
            d_shift_two.append(d_shift)
            d_scale_two.append(d_scale)
    with jax.named_scope("attention_grad"):
        image_dattn, text_dattn = rows_of_others(*gated_rows(d_middle, mods, 2))
        d_gate_one = [jnp.sum(d_middle[u] * attn[u], axis=1) for u in range(2)]
        text_dmixed = to_sequences(rows_dot(text_dattn, out_w[1][0]).astype(BF16), blocks)
        image_dmixed = [
            both(*[rows_dot(part, page).astype(BF16) for part in image_dattn]) for page in out_w[0]
        ]
        d_mixed = to_attention(image_dmixed, text_dmixed)
        tokens, columns = d_mixed.shape[1:]
        result = None
        if mlp is None:
            late, d_mixed = tied((saved["image_act"], saved["text_act"]), d_mixed)
            mlp, result = mlp_result(*late, down_w, middle, mods)
        d_mixed = lax.all_to_all(d_mixed, "dp", 0, 0, tiled=True)
        done = []
        if pending:
            mlp_before, d_mixed = tied(pending[0], d_mixed)
            done.append(mlp_shard(send_blocks(mlp_before, blocks)))
        d_mixed = d_mixed.reshape(-1, columns)
        d_packed = attention_backward(saved["packed"], d_mixed, saved["lse"])
        if pending:
            attn_before, d_packed = tied(pending[1], d_packed)
            attn_before = send_blocks(attn_before, blocks)
        d_packed = d_packed.reshape(-1, tokens, 3 * columns)
        d_packed = lax.all_to_all(d_packed, "dp", 0, 0, tiled=True)
        if pending:
            done[0], attn_before, d_packed = tied(done[0], attn_before, d_packed)
            done.append(attention_shard(attn_before))
        if result:
            mlp, result, d_packed = tied(mlp, result, d_packed)
        d_gate_two = [jnp.sum(grads_out[u] * mlp[u], axis=1) for u in range(2)]
        image_dproj, text_dproj = from_attention(d_packed, blocks, image_rows)
        text_dproj = to_blocks(text_dproj, seqs)
        grad_rows = image_dproj
        if not final:
            other = back_sum([part[seqs:] for part in image_dproj], qkv_w[0]).astype(BF16)
            grad_rows, other = tied(image_dproj, other)
        dattn_rows = both(*image_dattn)
        grads = page_list(
            [page_grad(saved["image_one"], part) for part in grad_rows],
            [page_grad(dattn_rows, part) for part in saved["image_mixed"]],
            page_grad(saved["text_one"], text_dproj),
            page_grad(text_dattn, saved["text_mixed"]),
        )
        wide = jnp.concatenate(grads, axis=1)
        if final:
            wide, image_dproj = tied(wide, image_dproj)
            other = back_sum([part[seqs:] for part in image_dproj], qkv_w[0]).astype(BF16)
        text_terms = back_dot(text_dproj, qkv_w[1][0])
        own = back_sum([part[:seqs] for part in image_dproj], qkv_w[0])
        (d_one,) = sum_over_others(own, other, text_terms)
        wide, mlp_slab = tied(wide, mlp_slab)
        attn_slab = scatter_pages(wide)
        d_inputs, d_mods = [], []
        for u in range(2):
            d_values, d_shift, d_scale = modulate_backward(
                saved["streams"][u], d_one[u], mods[u], 0
            )
            d_inputs.append(d_middle[u] + d_values)
            d_mods.append(
                jnp.concatenate(
                    [d_shift, d_scale, d_gate_one[u], d_shift_two[u], d_scale_two[u], d_gate_two[u]],
                    axis=1,
                )
            )
    return d_inputs, jnp.concatenate(d_mods), (mlp_slab, attn_slab), done, result


def with_blocks(pages):
    hi_count = lax.axis_size("tensor") // 2
    return [pages] + [hi_swap(pages, block) for block in range(1, hi_count)]


def gather_pages(pages):
    return lax.all_gather(pages, "dp", axis=1, tiled=True)


def attn_page(w_qkv, w_out, layer_at, u):
    qkv = w_qkv[layer_at, u].transpose(1, 0, 2)
    qkv = qkv.reshape(qkv.shape[0], -1)
    return jnp.concatenate([qkv, w_out[layer_at, u].T], axis=1)


def attention_shards(w_qkv, w_out, layer_at):
    return [attn_page(w_qkv, w_out, layer_at, u)[None] for u in range(2)]


def mlp_shards(w_up, w_down, layer_at):
    return [jnp.stack([w_up[layer_at, u], w_down[layer_at, u].T]) for u in range(2)]


def attention_pages(gathered):
    pages = [pages[at] for pages in gathered for at in range(pages.shape[0])]
    qkv_columns = pages[0].shape[1] * 3 // 4
    by_stream = [[pages[0], *pages[2:]], [pages[1]]]
    qkv_w = [[page[:, :qkv_columns] for page in group] for group in by_stream]
    out_w = [[page[:, qkv_columns:] for page in group] for group in by_stream]
    return qkv_w, out_w


def mlp_pages(gathered):
    pages = [pages[at] for pages in gathered for at in range(pages.shape[0])]
    by_stream = [[*pages[:2], *pages[4:]], pages[2:4]]
    return [group[0::2] for group in by_stream], [group[1::2] for group in by_stream]


def per_device(
    image_in,
    text_in,
    cond_table,
    cond_index,
    w_mod,
    w_qkv,
    w_out,
    w_up,
    w_down,
    cot_image,
    cot_text,
):
    n_tensor = lax.axis_size("tensor")
    dp_at = lax.axis_index("dp")
    micro_count, own_rows = image_in.shape[:2]
    seqs = micro_count * own_rows
    model_width = image_in.shape[3]
    layer_count = w_qkv.shape[0]
    slab_rows = w_mod.shape[2]
    column_count = w_mod.shape[3]
    index_flat = cond_index.reshape(-1)
    attn_shards = [attention_shards(w_qkv, w_out, at) for at in range(layer_count)]
    all_mlp_shards = [mlp_shards(w_up, w_down, at) for at in range(layer_count)]
    first_attn = gather_pages(jnp.concatenate(attn_shards[0], axis=0))
    with jax.named_scope("modulation"):
        onehot = (
            index_flat[:, None] == jnp.arange(cond_table.shape[0], dtype=jnp.int32)[None, :]
        ).astype(F32)
        cond_slab = lax.dynamic_slice_in_dim(cond_table, dp_at * slab_rows, slab_rows, 1)
        cond_slab = jnp.dot(onehot, cond_slab, precision=HIGHEST, preferred_element_type=F32)
        silu_slab = jax.nn.silu(cond_slab).astype(BF16)
        partial_mod = dot32("sd,lmdc->lmsc", silu_slab, w_mod)
        partial_mod = partial_mod.reshape(
            layer_count * 2, micro_count, n_tensor, own_rows * column_count
        )
        partial_mod = partial_mod.transpose(2, 0, 1, 3).reshape(n_tensor, -1, column_count)
        partial_mod = lax.all_to_all(partial_mod, "tensor", 0, 0, tiled=True)
        attn_own, partial_mod = tied(attn_shards[0], partial_mod)
        attn_others = with_blocks(attn_own[0])[1:]
        partial_mod = axis_sum(partial_mod, "dp")
        mod_own = partial_mod.transpose(1, 0, 2)
        mod_own = mod_own.reshape(layer_count, 2, seqs, 6, model_width)
    rest, first_attn, mod_own = tied(attn_others, first_attn, mod_own)
    attn_w = (first_attn, gather_pages(jnp.concatenate(rest, axis=0)))
    mods = [[mod_own[layer_at, u] for u in range(2)] for layer_at in range(layer_count)]

    def rows_in(values):
        return values.reshape(seqs, values.shape[2], model_width).astype(F32)

    def rows_out(values):
        return values.reshape(micro_count, own_rows, values.shape[1], model_width)

    streams = [rows_in(image_in), rows_in(text_in)]
    grads_now = [rows_in(cot_image), rows_in(cot_text)]
    saved, weights = [], []
    for layer_at in range(layer_count):
        last = layer_at + 1 == layer_count
        streams, kept, gathered, attn_w, dmlp = forward_layer(
            streams,
            mods[layer_at],
            attn_w,
            all_mlp_shards[layer_at],
            [] if last else attn_shards[layer_at + 1],
            gated_rows(grads_now, mods[layer_at], 5) if last else (),
        )
        weights.append(gathered)
        saved.append(kept)
    shards = [None] * layer_count
    d_mods = [None] * layer_count
    pending = None
    for layer_at in reversed(range(layer_count)):
        grads_now, d_mods[layer_at], slabs, done, result = backward_layer(
            grads_now,
            mods[layer_at],
            weights[layer_at],
            saved[layer_at],
            pending,
            layer_at == 0,
            dmlp,
        )
        dmlp = None
        streams = result or streams
        if pending:
            shards[layer_at + 1] = done
        pending = slabs
    with jax.named_scope("modulation_grad"):
        d_mods = jnp.concatenate(d_mods).reshape(layer_count * 2 * seqs, n_tensor, column_count)
        d_mods = lax.all_to_all(d_mods.transpose(1, 0, 2), "tensor", 0, 0, tiled=True)
        blocks = n_tensor // 2
        mlp_parts = send_blocks(pending[0], blocks)
        mlp_parts, attn_slab = tied(mlp_parts, pending[1])
        attn_parts = send_blocks(attn_slab, blocks)
        d_mods = axis_sum(d_mods, "dp")
        d_mods = d_mods.reshape(n_tensor, layer_count, 2, micro_count, own_rows, column_count)
        d_columns = d_mods.transpose(1, 2, 3, 0, 4, 5)
        d_columns = d_columns.reshape(layer_count, 2, -1, column_count)
        grad_w_mod = jnp.einsum(
            "sd,lmsc->lmdc",
            silu_slab.astype(F32),
            d_columns,
            precision=HIGHEST,
            preferred_element_type=F32,
        )
        d_silu = jnp.einsum(
            "lmsc,lmdc->sd",
            d_columns,
            w_mod.astype(F32),
            precision=HIGHEST,
            preferred_element_type=F32,
        )
    with jax.named_scope("conditioning_grad"):
        d_cond = jax.vjp(jax.nn.silu, cond_slab)[1](d_silu)[0]
        grad_cond = axis_sum(
            jnp.dot(onehot.T, d_cond, precision=HIGHEST, preferred_element_type=F32), "tensor"
        )
    with jax.named_scope("weight_grads"):
        mlp_done = [mlp_shard(mlp_parts)] + [layer[0] for layer in shards[1:]]
        grad_up, grad_down = [jnp.stack(parts) for parts in zip(*mlp_done)]
        attn_parts, grad_up, grad_down = tied(attn_parts, grad_up, grad_down)
        attn_done = [attention_shard(attn_parts)] + [layer[1] for layer in shards[1:]]
        grad_qkv, grad_out = [jnp.stack(parts) for parts in zip(*attn_done)]
    return (
        rows_out(streams[0].astype(BF16)),
        rows_out(streams[1].astype(BF16)),
        rows_out(grads_now[0]),
        rows_out(grads_now[1]),
        grad_cond,
        grad_w_mod,
        grad_qkv,
        grad_out,
        grad_up,
        grad_down,
    )


def solution(mesh):
    rows = P(None, "tensor", "dp", None)
    up_like = P(None, None, "dp", "tensor")
    down_like = P(None, None, "tensor", "dp")
    qkv_like = P(None, None, None, "dp", "tensor")
    return jax.shard_map(
        per_device,
        mesh=mesh,
        in_specs=(
            rows,
            rows,
            P(),
            P(),
            up_like,
            qkv_like,
            down_like,
            up_like,
            down_like,
            rows,
            rows,
        ),
        out_specs=(
            rows,
            rows,
            rows,
            rows,
            P(None, "dp"),
            up_like,
            qkv_like,
            down_like,
            up_like,
            down_like,
        ),
        check_vma=False,
    )
```
